256 devices in a mesh: tile: 16 (over x, y), mem: 16 (over z, core).
Axes of the slice: x: 4, y: 4, z: 8, core: 2. Of those that a mesh axis runs over, the one named last changes fastest.
Arguments:
- background_draws: float32 [64, 512, 1024], P('mem', 'tile'), may hold values from -6 to 6
- scaled_residuals: bfloat16 [64, 512, 1024], P('mem', 'tile'), may hold values from -6 to 6
- soil_site_tallies: int32 [16], P('tile'), may hold values from 1 to 4096, 40960 in all
- adjacent_patches: int32 [512, 9], P(('tile', 'mem')), may hold values from 0 to 512, as said below
- position_kinds: int32 [512, 9], P(('tile', 'mem')), may hold values from 0 to 8, as said below
Outputs:
- analysis: float32 [64, 512, 1024], P('mem', 'tile')
The draws below stay inside these ranges and needn't reach their ends.
Inputs may be any that keep to these rules, and one draw needn't show every extreme that they name: `adjacent_patches`: blocks form a grid of 64 rows by 8 columns, block id = row * 8 + column. Row b of neighbours lists distinct blocks among the 3 x 3 blocks around block b inside the grid, b itself always among them; the listed entries come first and the remaining slots hold 512. position_kinds[b, s] = 3 (dr + 1) + (dc + 1) where adjacent_patches[b, s] lies dr rows and dc columns from b; 4 in slots holding 512.
All inputs are finite; a program needn't handle non-finite values. No bound on the sum of `soil_site_tallies` on one device may be relied on, other than what follows from the above.
Results may differ from the reference program's by a relative error of at most 0.0039.
Values may be sent and summed in bfloat16 or wider, within the bound.
A program may use at most 64 MiB of HBM per device.

```python
import math
import jax
import jax.numpy as jnp
import numpy as np
from jax import lax

TRIAL_RUNS = 64
VARS = 8
BCELL = 128
CELL_COLS = 16
GC_HALF = 2
NB = 9
BCOLS = 8
BROWS = 4
BLK_TILE = 32
TILES = 16
PATCH_TOTAL = 512
PATCH_ENTRIES = 1024
CELLS_TILE = 4096


def neighbour_tables(key):
    grid_rows = TILES * BROWS
    block_ids = jnp.arange(PATCH_TOTAL, dtype=jnp.int32)
    block_row = block_ids // BCOLS
    block_col = block_ids % BCOLS
    slot_ids = jnp.arange(NB, dtype=jnp.int32)
    step_rows = slot_ids // 3 - 1
    step_cols = slot_ids % 3 - 1
    target_row = block_row[:, None] + step_rows[None, :]
    target_col = block_col[:, None] + step_cols[None, :]
    inside = (target_row >= 0) & (target_row < grid_rows) & (target_col >= 0) & (target_col < BCOLS)
    coastal = jax.random.randint(jax.random.fold_in(key, 7), (PATCH_TOTAL, NB), 0, 10) < 7
    forced = (block_ids == BLK_TILE + 1)[:, None] | (slot_ids == 4)[None, :]
    include = inside & (coastal | forced)
    order_key = jnp.where(include, slot_ids[None, :], slot_ids[None, :] + NB)
    ordering = jnp.argsort(order_key, axis=1, stable=True)
    target = target_row * BCOLS + target_col
    listed = jnp.where(include, target, PATCH_TOTAL)
    slot_kinds = jnp.where(include, slot_ids[None, :], 4)
    return (jnp.take_along_axis(listed, ordering, axis=1), jnp.take_along_axis(slot_kinds, ordering, axis=1))


def draw_adjacent_patches(key, part):
    return neighbour_tables(key)[0].astype(jnp.int32)


def draw_position_kinds(key, part):
    return neighbour_tables(key)[1].astype(jnp.int32)


def block_scale(stream_key, dims, split, least, largest):
    factor_of, own = 1.0, jax.random.fold_in(stream_key, 6)
    for position, parts in split:
        heights = jnp.exp(jax.random.uniform(jax.random.fold_in(own, position), (parts,), jnp.float32, least / len(split), largest / len(split)))
        factor_of = factor_of * jnp.repeat(heights, dims[position] // parts).reshape([-1 if axis == position else 1 for axis in range(len(dims))])
    return factor_of


def length_profile(amount, total, bound, slope):
    weights = [(1 << 20) // math.isqrt(rank ** slope) + 1 for rank in range(2, amount + 1)]
    spare, counts = total - bound - (amount - 1), [1] * (amount - 1)
    while spare > 0:
        movable = [i for i in range(amount - 1) if counts[i] < bound]
        mass, left = sum([weights[i] for i in movable]), spare
        for i in movable:
            more = min(bound - counts[i], max(1, left * weights[i] // mass), spare)
            counts[i] = counts[i] + more
            spare = spare - more
    return np.array([bound] + counts)


def uneven(key, amount, total, limit, skew):
    if amount == 2:
        one = jax.random.randint(key, (), max(1, total - limit), min(limit, total - 1) + 1)
        return jnp.stack([one, total - one])
    sizes = jnp.asarray(length_profile(amount, total, limit, skew), jnp.int32)
    twos = (amount - 1) // 2
    source_of, taker = sizes[1:1 + 2 * twos:2], sizes[2:2 + 2 * twos:2]
    margin = jnp.minimum(source_of - 1, limit - taker)
    passed = jax.random.randint(jax.random.fold_in(key, 1), (twos,), 0, 1 << 20) % (margin + 1)
    sizes = sizes.at[1:1 + 2 * twos:2].set(source_of - passed).at[2:2 + 2 * twos:2].set(taker + passed)
    return sizes[jax.random.permutation(jax.random.fold_in(key, 2), amount)]


def bell_draw(key, extent, spread, most, split=(), kind=jnp.bfloat16):
    values = spread * jax.random.normal(key, extent, jnp.float32)
    if split:
        values = values * block_scale(key, extent, split, -0.22, 0.18)
    return jnp.clip(values, -most, most).astype(kind)


def setup_inputs(seed: int = 0) -> dict:
    keys = jax.random.split(jax.random.key(seed), 6)
    return {
        "background_draws": bell_draw(keys[0], (TRIAL_RUNS, PATCH_TOTAL, PATCH_ENTRIES), 1.0, 6.0, ((0, 16), (1, 16)), jnp.float32),
        "scaled_residuals": bell_draw(keys[1], (TRIAL_RUNS, PATCH_TOTAL, PATCH_ENTRIES), 1.0, 6.0, ((0, 16), (1, 16))),
        "soil_site_tallies": uneven(keys[2], TILES, TILES * CELLS_TILE * 5 // 8, CELLS_TILE, 1).astype(jnp.int32),
        "adjacent_patches": draw_adjacent_patches(jax.random.fold_in(keys[5], 71), 0),
        "position_kinds": draw_position_kinds(jax.random.fold_in(keys[5], 71), 0),
    }


def taper_table(block_cells, cell_cols, half_cells):
    rows_block = block_cells // cell_cols
    half_width = float(half_cells)
    cell_ids = jnp.arange(block_cells)
    cell_row = (cell_ids // cell_cols).astype(jnp.float32)
    cell_col = (cell_ids % cell_cols).astype(jnp.float32)
    class_ids = jnp.arange(9)
    shift_rows = (class_ids // 3 - 1).astype(jnp.float32) * rows_block
    shift_cols = (class_ids % 3 - 1).astype(jnp.float32) * cell_cols
    delta_rows = shift_rows[:, None, None] + cell_row[None, None, :] - cell_row[None, :, None]
    delta_cols = shift_cols[:, None, None] + cell_col[None, None, :] - cell_col[None, :, None]
    scaled = jnp.sqrt(delta_rows * delta_rows + delta_cols * delta_cols) / half_width
    near_part = (((-0.25 * scaled + 0.5) * scaled + 0.625) * scaled - 5.0 / 3.0) * scaled * scaled + 1.0
    safe_scaled = jnp.maximum(scaled, 1.0)
    far_part = ((((scaled / 12.0 - 0.5) * scaled + 0.625) * scaled + 5.0 / 3.0) * scaled - 5.0) * scaled + 4.0 - 2.0 / (3.0 * safe_scaled)
    return jnp.where(scaled <= 1.0, near_part, jnp.where(scaled < 2.0, far_part, 0.0)).astype(jnp.float32)

def reference(background_draws, scaled_residuals, soil_site_tallies, adjacent_patches, position_kinds):
    expected_background_profile = lax.optimization_barrier(jnp.sum(background_draws, axis=0)) / TRIAL_RUNS
    block_ids = jnp.arange(PATCH_TOTAL, dtype=jnp.int32)
    tile_of = block_ids // BLK_TILE
    local_ids = block_ids % BLK_TILE
    cell_in = jnp.arange(PATCH_ENTRIES, dtype=jnp.int32) % BCELL
    ground_point_indicators = local_ids[:, None] * BCELL + cell_in[None, :] < soil_site_tallies[tile_of][:, None]
    trial_departures = jnp.where(ground_point_indicators[None], background_draws - expected_background_profile[None], 0.0).astype(jnp.bfloat16)
    padded_anom = jnp.concatenate([trial_departures, jnp.zeros((TRIAL_RUNS, 1, PATCH_ENTRIES), jnp.bfloat16)], axis=1)
    padded_innov = jnp.concatenate([scaled_residuals, jnp.zeros((TRIAL_RUNS, 1, PATCH_ENTRIES), jnp.bfloat16)], axis=1)
    taper = taper_table(BCELL, CELL_COLS, GC_HALF)

    def update_block(block_index):
        own_block = lax.dynamic_index_in_dim(trial_departures, block_index, 1, keepdims=False)

        def add_slot(slot_index, running):
            slot_index = jnp.asarray(slot_index).astype(jnp.int32)
            other_block = adjacent_patches[block_index, slot_index].astype(jnp.int32)
            taper_kind = position_kinds[block_index, slot_index].astype(jnp.int32)
            far_anom = lax.dynamic_index_in_dim(padded_anom, other_block, 1, keepdims=False)
            far_innov = lax.dynamic_index_in_dim(padded_innov, other_block, 1, keepdims=False)
            covariance = lax.dot_general(own_block, far_anom, (((0,), (0,)), ((), ())), preferred_element_type=jnp.float32)
            weights = taper[taper_kind]
            shaped = covariance.reshape(VARS, BCELL, VARS, BCELL) * weights[None, :, None, :]
            tapered = (shaped.reshape(PATCH_ENTRIES, PATCH_ENTRIES) / (TRIAL_RUNS - 1)).astype(jnp.bfloat16)
            return running + lax.dot_general(far_innov, tapered, (((1,), (1,)), ((), ())), preferred_element_type=jnp.float32)
        running = lax.fori_loop(0, NB, add_slot, jnp.zeros((TRIAL_RUNS, PATCH_ENTRIES), jnp.float32))
        return running.astype(jnp.bfloat16)
    correction_vectors = lax.map(update_block, block_ids)
    return background_draws + jnp.transpose(correction_vectors, (1, 0, 2)).astype(jnp.float32)
```

```python
import functools

import jax
import jax.numpy as jnp
import ml_dtypes
import numpy as np
from jax import lax
from jax.experimental import pallas as pl
from jax.experimental.pallas import tpu as pltpu
from jax.sharding import PartitionSpec as P

MESH = pl.DeviceIdType.MESH
F32 = jnp.float32
BF16 = jnp.bfloat16
W = 8
GROUPS = 16
NEAR = [1, 15, 2, 14, 3, 13, 4, 12, 5, 11, 6, 10, 7, 9, 8]


def taper_value(dy, dx):
    dy = np.asarray(dy, np.float32)
    dx = np.asarray(dx, np.float32)
    z = np.sqrt(dx * dx + dy * dy) / np.float32(2)
    near = (((np.float32(-0.25) * z + np.float32(0.5)) * z + np.float32(0.625)) * z - np.float32(5 / 3)) * z * z + 1
    safe = np.maximum(z, np.float32(1))
    far = (
        ((((z / np.float32(12) - np.float32(0.5)) * z + np.float32(0.625)) * z + np.float32(5 / 3)) * z - 5) * z
        + 4
        - np.float32(2) / (3 * safe)
    )
    return np.where(z <= 1, near, np.where(z < 2, far, 0)).astype(np.float32)


def side_slots():
    tiles = [[], [], []]
    for row in range(16):
        for depth in (1, 2, 3):
            tile = 0 if row < 5 else 2 if row > 10 else 1
            if row == 5 and depth == 3:
                tile = 0
            if row == 10 and depth == 3:
                tile = 2
            tiles[tile] += [(row, depth, w) for w in range(W)]
    return tiles


def vert_slots():
    return [(row, col, w) for w in range(W) for row in range(3) for col in range(16)]


def corner_slots():
    return [(a, b, w) for a in (1, 2, 3) for b in (1, 2, 3) if (a, b) != (3, 3) for w in range(W)]


def tables():
    sides, vert, corner = side_slots(), vert_slots(), corner_slots()
    select = np.zeros((2, 1024, 1408), np.float32)

    def put(lane, part, row, col, w):
        block, in_row = divmod(row, 8)
        if part is None or block == part:
            select[block, w * 128 + in_row * 16 + col, lane] = 1

    for lane, (row, col, w) in enumerate(vert):
        put(lane, 0, row, col, w)
        put(384 + lane, 0, 5 + row, col, w)
        put(lane, 1, 13 + row, col, w)
        put(384 + lane, 1, 8 + row, col, w)
    for tile in range(3):
        for lane, (row, depth, w) in enumerate(sides[tile]):
            block = row // 8
            at = 768 + (tile - block) * 128 + lane
            put(at, block, row, depth - 1, w)
            put(at + 256, block, row, 16 - depth, w)
    for lane, (a, b, w) in enumerate(corner):
        put(1280 + lane, 0, a - 1, 16 - b, w)
        put(1344 + lane, 0, a - 1, b - 1, w)
        put(1280 + lane, 1, 16 - a, 16 - b, w)
        put(1344 + lane, 1, 16 - a, b - 1, w)

    weights = np.zeros((4, 64, 1024), np.float32)
    kinds = np.full((4, 1024), 4, np.int32)
    self_weights = np.zeros((2, 64, 128), np.float32)
    cell = np.arange(64)
    for s in range(4):
        block = s // 2
        own_row, own_col = 4 * s + cell // 16, cell % 16
        slots = [None] * 1024
        base = [-3, 8, 5, 16][s]
        for lane, (row, col, w) in enumerate(vert):
            slots[lane] = (base + row, col)
        if s in (0, 3):
            for lane, (a, b, w) in enumerate(corner):
                row = -a if s == 0 else 15 + a
                slots[384 + lane] = (row, -b)
                slots[448 + lane] = (row, 15 + b)
        for k in range(2):
            for lane, (row, depth, w) in enumerate(sides[k + (s >= 2)]):
                slots[512 + 128 * k + lane] = (row, -depth)
                slots[768 + 128 * k + lane] = (row, 15 + depth)
        for lane, slot in enumerate(slots):
            if slot is not None:
                row, col = slot
                weights[s, :, lane] = taper_value(row - own_row, col - own_col) / np.float32(63)
                kinds[s, lane] = 3 * (row // 8 - block + 1) + col // 16 + 1
        if s < 2:
            every = np.arange(128)
            self_weights[s] = taper_value(
                (every // 16)[None] - own_row[:, None], (every % 16)[None] - own_col[:, None]
            ) / np.float32(63)
    return select.astype(ml_dtypes.bfloat16), weights, kinds, self_weights


UP, DN, TL, TR, CU, CD = 0, 384, 768, 1152, 1536, 1664
VUP, VDN, LEFT, RIGHT, CUL, CUR, CDL, CDR = 0, 384, 768, 1152, 1536, 1664, 1792, 1920


def kernel(
    bg_ref, inn_ref, tally_ref, kinds_ref, region_ref, selfw_ref, sel_hbm, weight_hbm,
    out_ref,
    sel, weight, mask_out, mask_in, ha, hl, hi, stage, ca, ci, ra, ri, fa, fi, xa, xi, at, hsa, hsi, rha, rhi,
    inner, exta, exti, tt, acc, rs, cb, rb, fb,
    const_sem, mask_send, mask_recv, as_, ar_, is_, ir_, hs_, hr_, gs_, gr_, bs_, br_,
):
    t = lax.axis_index("tile")
    me = lax.axis_index("mem")
    z, c = me // 2, me % 2
    left, right = 2 * ((z + 7) % 8), 2 * ((z + 1) % 8)
    up_tile, down_tile = (t + 15 + c) % 16, (t + c) % 16
    other = 1 - c

    across = (t + 15 + 2 * c) % 16
    barrier = pltpu.get_barrier_semaphore()
    for k in range(1, GROUPS):
        pl.semaphore_signal(barrier, inc=1, device_id=(t, (me + k) % GROUPS), device_id_type=MESH)
    for base in (left, 2 * z, right):
        pl.semaphore_signal(barrier, inc=1, device_id=(across, base + other), device_id_type=MESH)

    load_sel = pltpu.make_async_copy(sel_hbm, sel, const_sem.at[0])
    load_weight = pltpu.make_async_copy(weight_hbm, weight, const_sem.at[1])
    load_sel.start()
    load_weight.start()

    lane8 = lax.broadcasted_iota(jnp.int32, (8, 128), 1)
    for q in range(2):
        held = jnp.where(lane8 == 4, 1.0, 0.0)
        for s in range(9):
            held = jnp.where(kinds_ref[q : q + 1, s : s + 1] == lane8, 1.0, held)
        mask_out[q] = held

    for r in range(4):
        rows = slice(8 * r, 8 * r + 8)
        for w in range(W):
            lanes = slice(128 * w, 128 * w + 128)
            x0, x1, x2, x3 = (bg_ref[m, rows, lanes] for m in range(4))
            s01, d01, s23, d23 = x0 + x1, x0 - x1, x2 + x3, x2 - x3
            h0 = (s01 + s23) * 0.5
            high = h0.astype(BF16).astype(F32)
            base = (r // 2) * 64 + (r % 2) * 8
            ha[w, base : base + 8, :] = high
            ha[w, base + 16 : base + 24, :] = (s01 - s23) * 0.5
            ha[w, base + 32 : base + 40, :] = (d01 + d23) * 0.5
            ha[w, base + 48 : base + 56, :] = (d01 - d23) * 0.5
            hl[w, rows, :] = h0 - high
    for w in range(W):
        for m in range(4):
            y = inn_ref[m, :, 128 * w : 128 * w + 128].astype(F32)
            for r in range(4):
                base = (r // 2) * 64 + m * 16 + (r % 2) * 8
                hi[w, base : base + 8, :] = y[8 * r : 8 * r + 8, :]

    def build(dest, carry):
        col, core = dest // 2, dest % 2
        for w in range(0, W, 2):
            for source, chunk in ((ha, ca), (hi, ci)):
                a = source[w, pl.ds(core * 64 + col, 8, stride=8), :]
                b = source[w + 1, pl.ds(core * 64 + col, 8, stride=8), :]
                chunk[dest, 8 * w : 8 * w + 16, :] = jnp.concatenate([a, b], axis=0).astype(BF16)
        for w in range(W):
            stage[2 * w : 2 * w + 2, :] = hl[w, pl.ds(core * 16 + col, 2, stride=8), :]
        ca[dest, 64:80, :] = stage[...].astype(BF16)
        return carry

    lax.fori_loop(0, GROUPS, build, 0)

    pl.semaphore_wait(barrier, GROUPS + 2)

    mask_row = me // 4

    def mask_copy(q):
        target = 2 * (2 * (me % 4) + q) + mask_row // 2
        return target, pltpu.make_async_remote_copy(
            src_ref=mask_out.at[q], dst_ref=mask_in.at[mask_row % 2], send_sem=mask_send.at[q],
            recv_sem=mask_recv.at[mask_row % 2], device_id=(t, target), device_id_type=MESH,
        )

    for q in range(2):
        target, copy = mask_copy(q)

        @pl.when(target != me)
        def _(copy=copy):
            copy.start()

        @pl.when(target == me)
        def _(q=q):
            mask_in[mask_row % 2] = mask_out[q]

    def spread(source, landing, send, recv):
        copies = {}
        for k in NEAR:
            peer = (me + k) % GROUPS
            copies[k] = pltpu.make_async_remote_copy(
                src_ref=source.at[peer], dst_ref=landing.at[me], send_sem=send.at[k], recv_sem=recv.at[k],
                device_id=(t, peer), device_id_type=MESH,
            )
            copies[k].start()
        return copies

    a_copies = spread(ca, ra, as_, ar_)
    i_copies = spread(ci, ri, is_, ir_)

    load_sel.wait()
    load_weight.wait()
    for b in range(2):
        @pl.when(4 * (2 * c + b) + z // 2 != me)
        def _(b=b):
            pltpu.make_async_remote_copy(
                src_ref=mask_out.at[0], dst_ref=mask_in.at[b], send_sem=mask_send.at[0], recv_sem=mask_recv.at[b],
                device_id=(t, (me + 1) % GROUPS), device_id_type=MESH,
            ).wait_recv()

    for s in range(4):
        block = s // 2
        region = region_ref[s : s + 1, :]
        row = jnp.zeros((1, 1024), F32)
        for k in ((0, 1, 2, 3, 5), (3, 5, 6, 7, 8), (0, 1, 2, 3, 5), (3, 5, 6, 7, 8))[s]:
            row = jnp.where(region == k, mask_in[block, 0:1, k : k + 1], row)
        weight[s] = weight[s] * row

    def halo(hs, rh, send, recv):
        plan = [
            (UP, VDN, 384, (up_tile, 2 * z + other), 1),
            (DN, VUP, 384, (down_tile, 2 * z + other), 0),
            (TL, RIGHT, 384, (t, left + c), 3),
            (TR, LEFT, 384, (t, right + c), 2),
            (CU, CDL, 128, (up_tile, right + other), 6),
            (CU, CDR, 128, (up_tile, left + other), 7),
            (CD, CUL, 128, (down_tile, right + other), 4),
            (CD, CUR, 128, (down_tile, left + other), 5),
        ]
        copies = []
        for source, landing, width, device, n in plan:
            copy = pltpu.make_async_remote_copy(
                src_ref=hs.at[:, source : source + width], dst_ref=rh.at[:, landing : landing + width],
                send_sem=send.at[n], recv_sem=recv.at[n], device_id=device, device_id_type=MESH,
            )
            copy.start()
            copies.append(copy)
        return copies

    def pick(x, hs, inner_at):
        m0 = jnp.dot(x[0], sel[0], preferred_element_type=F32)
        m1 = jnp.dot(x[1], sel[1], preferred_element_type=F32)
        hs[:, UP : UP + 384] = m0[:, 0:384].astype(BF16)
        hs[:, DN : DN + 384] = m1[:, 0:384].astype(BF16)
        for k, place in enumerate((TL, TR)):
            at0 = 768 + 256 * k
            hs[:, place : place + 128] = m0[:, at0 : at0 + 128].astype(BF16)
            hs[:, place + 128 : place + 256] = (m0[:, at0 + 128 : at0 + 256] + m1[:, at0 : at0 + 128]).astype(BF16)
            hs[:, place + 256 : place + 384] = m1[:, at0 + 128 : at0 + 256].astype(BF16)
        hs[:, CU : CU + 128] = m0[:, 1280:1408].astype(BF16)
        hs[:, CD : CD + 128] = m1[:, 1280:1408].astype(BF16)
        inner[inner_at, 0] = m1[:, 384:768].astype(BF16)
        inner[inner_at, 1] = m0[:, 384:768].astype(BF16)

    def assemble(rh, ext, inner_at):
        first = lax.broadcasted_iota(jnp.int32, (64, 128), 1) < 64
        verts = (rh[:, VUP : VUP + 384], inner[inner_at, 0], inner[inner_at, 1], rh[:, VDN : VDN + 384])
        above = jnp.where(first, rh[:, CUL : CUL + 128].astype(F32), rh[:, CUR : CUR + 128].astype(F32)).astype(BF16)
        below = jnp.where(first, rh[:, CDL : CDL + 128].astype(F32), rh[:, CDR : CDR + 128].astype(F32)).astype(BF16)
        for s in range(4):
            shift = 128 * (s // 2)
            ext[s, :, 0:384] = verts[s]
            ext[s, :, 384:512] = above if s < 2 else below
            ext[s, :, 512:768] = rh[:, LEFT + shift : LEFT + shift + 256]
            ext[s, :, 768:1024] = rh[:, RIGHT + shift : RIGHT + shift + 256]

    fa[pl.ds(pl.multiple_of(me * 80, 8), 80), :] = ca[me].astype(F32)
    for k in NEAR:
        a_copies[k].wait_recv()
        g = (me + GROUPS - k) % GROUPS
        fa[pl.ds(pl.multiple_of(g * 80, 8), 80), :] = ra[g].astype(F32)
    cell = lax.broadcasted_iota(jnp.int32, (1, 128), 1)
    for b in range(2):
        land = jnp.where((8 * (2 * c + b) + z) * 128 + cell < tally_ref[0], 1.0, 0.0)
        for w in range(W):
            lanes = slice(128 * w, 128 * w + 128)
            h0 = fa[pl.ds(8 * w + b, 16, stride=80), :] + fa[pl.ds(64 + 2 * w + b, 16, stride=80), :]
            parts = [h0 - jnp.sum(h0, axis=0, keepdims=True) * (1.0 / GROUPS)]
            parts += [fa[pl.ds(8 * w + 2 * m + b, 16, stride=80), :] for m in (1, 2, 3)]
            tile = jnp.concatenate(parts, axis=0) * land
            xa[b, :, lanes] = tile.astype(BF16)
            turned = tile.T.astype(BF16)
            at[2 * b, 64 * w : 64 * w + 64, :] = turned[0:64]
            at[2 * b + 1, 64 * w : 64 * w + 64, :] = turned[64:128]
    pick(xa, hsa, 0)
    ha_copies = halo(hsa, rha, hs_, hr_)

    def own_taper(s, carry):
        rows = at[s]
        table = selfw_ref[s % 2]
        for n in range(4):
            cov = jnp.dot(rows, xa[s // 2, :, 256 * n : 256 * n + 256], preferred_element_type=F32)
            for h in range(2):
                part = cov[:, 128 * h : 128 * h + 128].reshape(W, 64, 128) * table[None]
                lanes = slice(256 * n + 128 * h, 256 * n + 128 * h + 128)
                tt[s, 0, :, lanes] = part.reshape(512, 128).astype(BF16)
        return carry

    lax.fori_loop(0, 4, own_taper, 0)
    for copy in ha_copies:
        copy.wait_recv()
    assemble(rha, exta, 0)

    def halo_taper(s, carry):
        rows = at[s]
        for n in range(4):
            lanes = slice(256 * n, 256 * n + 256)
            cov = jnp.dot(rows, exta[s, :, lanes], preferred_element_type=F32)
            part = cov.reshape(W, 64, 256) * weight[s, :, lanes][None]
            tt[s, 1, :, lanes] = part.reshape(512, 256).astype(BF16)
        return carry

    lax.fori_loop(0, 4, halo_taper, 0)

    fi[pl.ds(pl.multiple_of(me * 64, 8), 64), :] = ci[me].astype(F32)
    for k in NEAR:
        i_copies[k].wait_recv()
        g = (me + GROUPS - k) % GROUPS
        fi[pl.ds(pl.multiple_of(g * 64, 8), 64), :] = ri[g].astype(F32)
    for b in range(2):
        for w in range(W):
            parts = [fi[pl.ds(8 * w + 2 * m + b, 16, stride=64), :] for m in range(4)]
            xi[b, :, 128 * w : 128 * w + 128] = jnp.concatenate(parts, axis=0).astype(BF16)
    pick(xi, hsi, 1)
    hi_copies = halo(hsi, rhi, gs_, gr_)

    contract = (((1,), (1,)), ((), ()))

    def own_update(s, carry):
        acc[s] = lax.dot_general(tt[s, 0], xi[s // 2], contract, preferred_element_type=F32)
        return carry

    lax.fori_loop(0, 4, own_update, 0)
    for copy in hi_copies:
        copy.wait_recv()
    assemble(rhi, exti, 1)

    def halo_update(s, carry):
        acc[s] = acc[s] + lax.dot_general(tt[s, 1], exti[s], contract, preferred_element_type=F32)
        return carry

    back = {}
    for b in range(2):
        lax.fori_loop(2 * b, 2 * b + 2, halo_update, 0)
        for w in range(W):
            rows = slice(64 * w, 64 * w + 64)
            tile = jnp.concatenate([acc[2 * b, rows, :], acc[2 * b + 1, rows, :]], axis=0).T
            at0 = (8 * b + w) * 64
            rs[at0 : at0 + 64, :] = tile

        def chunk(g, carry, b=b):
            cb[g, b] = rs[pl.ds(512 * b + g, 32, stride=16), :].astype(BF16)
            return carry

        lax.fori_loop(0, GROUPS, chunk, 0)
        for k in NEAR:
            peer = (me + k) % GROUPS
            back[b, k] = pltpu.make_async_remote_copy(
                src_ref=cb.at[peer, b], dst_ref=rb.at[me, b], send_sem=bs_.at[b, k], recv_sem=br_.at[b, k],
                device_id=(t, peer), device_id_type=MESH,
            )
            back[b, k].start()

    for b in range(2):
        fb[pl.ds(pl.multiple_of(me * 64 + 32 * b, 8), 32), :] = cb[me, b].astype(F32)
        for k in NEAR:
            back[b, k].wait_recv()
            g = (me + GROUPS - k) % GROUPS
            fb[pl.ds(pl.multiple_of(g * 64 + 32 * b, 8), 32), :] = rb[g, b].astype(F32)
    for m in range(4):
        for r in range(4):
            rows = slice(8 * r, 8 * r + 8)
            for w in range(W):
                lanes = slice(128 * w, 128 * w + 128)
                update = fb[pl.ds((r // 2) * 64 + (r % 2) * 32 + 4 * w + m, 8, stride=128), :]
                out_ref[m, rows, lanes] = bg_ref[m, rows, lanes] + update

    for copies in (a_copies, i_copies, back):
        for copy in copies.values():
            copy.wait_send()
    for copy in ha_copies + hi_copies:
        copy.wait_send()
    for q in range(2):
        target, copy = mask_copy(q)

        @pl.when(target != me)
        def _(copy=copy):
            copy.wait_send()


def local(background_draws, scaled_residuals, soil_site_tallies, adjacent_patches, position_kinds):
    select, weights, kinds, self_weights = tables()
    vmem = pl.BlockSpec(memory_space=pltpu.VMEM)
    anywhere = pl.BlockSpec(memory_space=pl.ANY)
    sems = pltpu.SemaphoreType.DMA
    return pl.pallas_call(
        kernel,
        out_shape=jax.ShapeDtypeStruct(background_draws.shape, F32),
        in_specs=[vmem, vmem, pl.BlockSpec(memory_space=pltpu.SMEM), vmem, vmem, vmem, anywhere, anywhere],
        out_specs=vmem,
        scratch_shapes=[
            pltpu.VMEM((2, 1024, 1408), BF16),
            pltpu.VMEM((4, 64, 1024), F32),
            pltpu.VMEM((2, 8, 128), F32),
            pltpu.VMEM((2, 8, 128), F32),
            pltpu.VMEM((W, 128, 128), F32),
            pltpu.VMEM((W, 32, 128), F32),
            pltpu.VMEM((W, 128, 128), F32),
            pltpu.VMEM((16, 128), F32),
            pltpu.VMEM((GROUPS, 80, 128), BF16),
            pltpu.VMEM((GROUPS, 64, 128), BF16),
            pltpu.VMEM((GROUPS, 80, 128), BF16),
            pltpu.VMEM((GROUPS, 64, 128), BF16),
            pltpu.VMEM((GROUPS * 80, 128), F32),
            pltpu.VMEM((GROUPS * 64, 128), F32),
            pltpu.VMEM((2, 64, 1024), BF16),
            pltpu.VMEM((2, 64, 1024), BF16),
            pltpu.VMEM((4, 512, 64), BF16),
            pltpu.VMEM((64, 1792), BF16),
            pltpu.VMEM((64, 1792), BF16),
            pltpu.VMEM((64, 2048), BF16),
            pltpu.VMEM((64, 2048), BF16),
            pltpu.VMEM((2, 2, 64, 384), BF16),
            pltpu.VMEM((4, 64, 1024), BF16),
            pltpu.VMEM((4, 64, 1024), BF16),
            pltpu.VMEM((4, 2, 512, 1024), BF16),
            pltpu.VMEM((4, 512, 64), F32),
            pltpu.VMEM((1024, 128), F32),
            pltpu.VMEM((GROUPS, 2, 32, 128), BF16),
            pltpu.VMEM((GROUPS, 2, 32, 128), BF16),
            pltpu.VMEM((GROUPS * 64, 128), F32),
            sems((2,)), sems((2,)), sems((2,)),
            sems((GROUPS,)), sems((GROUPS,)), sems((GROUPS,)), sems((GROUPS,)),
            sems((8,)), sems((8,)), sems((8,)), sems((8,)),
            sems((2, GROUPS)), sems((2, GROUPS)),
        ],
        compiler_params=pltpu.CompilerParams(
            collective_id=0, has_side_effects=True, vmem_limit_bytes=56 * 2**20
        ),
    )(
        background_draws, scaled_residuals, soil_site_tallies, position_kinds,
        jnp.asarray(kinds), jnp.asarray(self_weights), jnp.asarray(select), jnp.asarray(weights),
    )


def solution(mesh):
    in_specs = (
        P("mem", "tile", None),
        P("mem", "tile", None),
        P("tile"),
        P(("tile", "mem"), None),
        P(("tile", "mem"), None),
    )
    out_specs = P("mem", "tile", None)
    return jax.shard_map(local, mesh=mesh, in_specs=in_specs, out_specs=out_specs, check_vma=False)
```

```python
import functools

import jax
import jax.numpy as jnp
import numpy as np
from jax import lax
from jax.experimental import pallas as pl
from jax.experimental.pallas import tpu as pltpu
from jax.sharding import PartitionSpec as P

MESH = pl.DeviceIdType.MESH
F32 = jnp.float32
BF16 = jnp.bfloat16
W = 8
GROUPS = 16
NEAR = [1, 15, 2, 14, 3, 13, 4, 12, 5, 11, 6, 10, 7, 9, 8]


def taper_value(dy, dx):
    dy = np.asarray(dy, np.float32)
    dx = np.asarray(dx, np.float32)
    z = np.sqrt(dx * dx + dy * dy) / np.float32(2)
    near = (((np.float32(-0.25) * z + np.float32(0.5)) * z + np.float32(0.625)) * z - np.float32(5 / 3)) * z * z + 1
    safe = np.maximum(z, np.float32(1))
    far = (
        ((((z / np.float32(12) - np.float32(0.5)) * z + np.float32(0.625)) * z + np.float32(5 / 3)) * z - 5) * z
        + 4
        - np.float32(2) / (3 * safe)
    )
    return np.where(z <= 1, near, np.where(z < 2, far, 0)).astype(np.float32)


def side_slots():
    tiles = [[], [], []]
    for row in range(16):
        for depth in (1, 2, 3):
            tile = 0 if row < 5 else 2 if row > 10 else 1
            if row == 5 and depth == 3:
                tile = 0
            if row == 10 and depth == 3:
                tile = 2
            tiles[tile] += [(row, depth, w) for w in range(W)]
    return tiles


def vert_slots():
    return [(row, col, w) for w in range(W) for row in range(3) for col in range(16)]


def corner_slots():
    return [(a, b, w) for a in (1, 2, 3) for b in (1, 2, 3) if (a, b) != (3, 3) for w in range(W)]


def tables():
    sides, vert, corner = side_slots(), vert_slots(), corner_slots()
    select = np.full((2, 1408), -1, np.int32)

    def put(lane, part, row, col, w):
        block, in_row = divmod(row, 8)
        if part is None or block == part:
            select[block, lane] = w * 128 + in_row * 16 + col

    for lane, (row, col, w) in enumerate(vert):
        put(lane, 0, row, col, w)
        put(384 + lane, 0, 5 + row, col, w)
        put(lane, 1, 13 + row, col, w)
        put(384 + lane, 1, 8 + row, col, w)
    for tile in range(3):
        for lane, (row, depth, w) in enumerate(sides[tile]):
            block = row // 8
            at = 768 + (tile - block) * 128 + lane
            put(at, block, row, depth - 1, w)
            put(at + 256, block, row, 16 - depth, w)
    for lane, (a, b, w) in enumerate(corner):
        put(1280 + lane, 0, a - 1, 16 - b, w)
        put(1344 + lane, 0, a - 1, b - 1, w)
        put(1280 + lane, 1, 16 - a, 16 - b, w)
        put(1344 + lane, 1, 16 - a, b - 1, w)

    weights = np.zeros((4, 64, 1024), np.float32)
    kinds = np.full((4, 1024), 4, np.int32)
    self_weights = np.zeros((2, 64, 128), np.float32)
    cell = np.arange(64)
    for s in range(4):
        block = s // 2
        own_row, own_col = 4 * s + cell // 16, cell % 16
        slots = [None] * 1024
        base = [-3, 8, 5, 16][s]
        for lane, (row, col, w) in enumerate(vert):
            slots[lane] = (base + row, col)
        if s in (0, 3):
            for lane, (a, b, w) in enumerate(corner):
                row = -a if s == 0 else 15 + a
                slots[384 + lane] = (row, -b)
                slots[448 + lane] = (row, 15 + b)
        for k in range(2):
            for lane, (row, depth, w) in enumerate(sides[k + (s >= 2)]):
                slots[512 + 128 * k + lane] = (row, -depth)
                slots[768 + 128 * k + lane] = (row, 15 + depth)
        for lane, slot in enumerate(slots):
            if slot is not None:
                row, col = slot
                weights[s, :, lane] = taper_value(row - own_row, col - own_col) / np.float32(63)
                kinds[s, lane] = 3 * (row // 8 - block + 1) + col // 16 + 1
        if s < 2:
            every = np.arange(128)
            self_weights[s] = taper_value(
                (every // 16)[None] - own_row[:, None], (every % 16)[None] - own_col[:, None]
            ) / np.float32(63)
    return select, weights, kinds, self_weights


UP, DN, TL, TR, CU, CD = 0, 384, 768, 1152, 1536, 1664
VUP, VDN, LEFT, RIGHT, CUL, CUR, CDL, CDR = 0, 384, 768, 1152, 1536, 1664, 1792, 1920


def kernel(
    bg_ref, inn_ref, tally_ref, kinds_ref, region_ref, selfw_ref, select_ref, weight_hbm,
    out_ref,
    sel, weight, mask_out, mask_in, ha, hl, hi, stage, ca, ci, ra, ri, fa, fi, xa, xi, at, hsa, hsi, rha, rhi,
    inner, exta, exti, tt, acc, rs, cb, rb, fb,
    const_sem, mask_send, mask_recv, as_, ar_, is_, ir_, hs_, hr_, gs_, gr_, bs_, br_,
):
    t = lax.axis_index("tile")
    me = lax.axis_index("mem")
    z, c = me // 2, me % 2
    left, right = 2 * ((z + 7) % 8), 2 * ((z + 1) % 8)
    up_tile, down_tile = (t + 15 + c) % 16, (t + c) % 16
    other = 1 - c

    across = (t + 15 + 2 * c) % 16
    barrier = pltpu.get_barrier_semaphore()
    for k in range(1, GROUPS):
        pl.semaphore_signal(barrier, inc=1, device_id=(t, (me + k) % GROUPS), device_id_type=MESH)
    for base in (left, 2 * z, right):
        pl.semaphore_signal(barrier, inc=1, device_id=(across, base + other), device_id_type=MESH)

    load_weight = pltpu.make_async_copy(weight_hbm, weight, const_sem)
    load_weight.start()

    lane8 = lax.broadcasted_iota(jnp.int32, (8, 128), 1)
    for q in range(2):
        held = jnp.where(lane8 == 4, 1.0, 0.0)
        for s in range(9):
            held = jnp.where(kinds_ref[q : q + 1, s : s + 1] == lane8, 1.0, held)
        mask_out[q] = held

    for r in range(4):
        rows = slice(8 * r, 8 * r + 8)
        for w in range(W):
            lanes = slice(128 * w, 128 * w + 128)
            x0, x1, x2, x3 = (bg_ref[m, rows, lanes] for m in range(4))
            s01, d01, s23, d23 = x0 + x1, x0 - x1, x2 + x3, x2 - x3
            h0 = (s01 + s23) * 0.5
            high = h0.astype(BF16).astype(F32)
            base = (r // 2) * 64 + (r % 2) * 8
            ha[w, base : base + 8, :] = high
            ha[w, base + 16 : base + 24, :] = (s01 - s23) * 0.5
            ha[w, base + 32 : base + 40, :] = (d01 + d23) * 0.5
            ha[w, base + 48 : base + 56, :] = (d01 - d23) * 0.5
            hl[w, rows, :] = h0 - high
    for w in range(W):
        for m in range(4):
            y = inn_ref[m, :, 128 * w : 128 * w + 128].astype(F32)
            for r in range(4):
                base = (r // 2) * 64 + m * 16 + (r % 2) * 8
                hi[w, base : base + 8, :] = y[8 * r : 8 * r + 8, :]

    def build(dest, carry):
        col, core = dest // 2, dest % 2
        for w in range(0, W, 2):
            for source, chunk in ((ha, ca), (hi, ci)):
                a = source[w, pl.ds(core * 64 + col, 8, stride=8), :]
                b = source[w + 1, pl.ds(core * 64 + col, 8, stride=8), :]
                chunk[dest, 8 * w : 8 * w + 16, :] = jnp.concatenate([a, b], axis=0).astype(BF16)
        for w in range(W):
            stage[2 * w : 2 * w + 2, :] = hl[w, pl.ds(core * 16 + col, 2, stride=8), :]
        ca[dest, 64:80, :] = stage[...].astype(BF16)
        return carry

    lax.fori_loop(0, GROUPS, build, 0)

    pl.semaphore_wait(barrier, GROUPS + 2)

    mask_row = me // 4

    def mask_copy(q):
        target = 2 * (2 * (me % 4) + q) + mask_row // 2
        return target, pltpu.make_async_remote_copy(
            src_ref=mask_out.at[q], dst_ref=mask_in.at[mask_row % 2], send_sem=mask_send.at[q],
            recv_sem=mask_recv.at[mask_row % 2], device_id=(t, target), device_id_type=MESH,
        )

    for q in range(2):
        target, copy = mask_copy(q)

        @pl.when(target != me)
        def _(copy=copy):
            copy.start()

        @pl.when(target == me)
        def _(q=q):
            mask_in[mask_row % 2] = mask_out[q]

    def spread(source, landing, send, recv, start=0, size=80):
        copies = {}
        for k in NEAR:
            peer = (me + k) % GROUPS
            copies[k] = pltpu.make_async_remote_copy(
                src_ref=source.at[peer, pl.ds(start, size)], dst_ref=landing.at[me, pl.ds(start, size)],
                send_sem=send.at[k], recv_sem=recv.at[k], device_id=(t, peer), device_id_type=MESH,
            )
            copies[k].start()
        return copies

    a_copies = spread(ca, ra, as_, ar_)
    i_copies = spread(ci, ri, is_, ir_, 0, 64)

    for b in range(2):
        wanted = select_ref[b : b + 1, :]

        def one_hot(k, carry, b=b, wanted=wanted):
            entry = lax.broadcasted_iota(jnp.int32, (128, 1408), 0) + 128 * k
            sel[b, pl.ds(pl.multiple_of(128 * k, 128), 128), :] = jnp.where(entry == wanted, 1.0, 0.0).astype(BF16)
            return carry

        lax.fori_loop(0, 8, one_hot, 0)

    def halo(hs, rh, send, recv):
        plan = [
            (UP, VDN, 384, (up_tile, 2 * z + other), 1),
            (DN, VUP, 384, (down_tile, 2 * z + other), 0),
            (TL, RIGHT, 384, (t, left + c), 3),
            (TR, LEFT, 384, (t, right + c), 2),
            (CU, CDL, 128, (up_tile, right + other), 6),
            (CU, CDR, 128, (up_tile, left + other), 7),
            (CD, CUL, 128, (down_tile, right + other), 4),
            (CD, CUR, 128, (down_tile, left + other), 5),
        ]
        copies = []
        for source, landing, width, device, n in plan:
            copy = pltpu.make_async_remote_copy(
                src_ref=hs.at[:, source : source + width], dst_ref=rh.at[:, landing : landing + width],
                send_sem=send.at[n], recv_sem=recv.at[n], device_id=device, device_id_type=MESH,
            )
            copy.start()
            copies.append(copy)
        return copies

    def pick(x, hs, inner_at):
        m0 = jnp.dot(x[0], sel[0], preferred_element_type=F32)
        m1 = jnp.dot(x[1], sel[1], preferred_element_type=F32)
        hs[:, UP : UP + 384] = m0[:, 0:384].astype(BF16)
        hs[:, DN : DN + 384] = m1[:, 0:384].astype(BF16)
        for k, place in enumerate((TL, TR)):
            at0 = 768 + 256 * k
            hs[:, place : place + 128] = m0[:, at0 : at0 + 128].astype(BF16)
            hs[:, place + 128 : place + 256] = (m0[:, at0 + 128 : at0 + 256] + m1[:, at0 : at0 + 128]).astype(BF16)
            hs[:, place + 256 : place + 384] = m1[:, at0 + 128 : at0 + 256].astype(BF16)
        hs[:, CU : CU + 128] = m0[:, 1280:1408].astype(BF16)
        hs[:, CD : CD + 128] = m1[:, 1280:1408].astype(BF16)
        inner[inner_at, 0] = m1[:, 384:768].astype(BF16)
        inner[inner_at, 1] = m0[:, 384:768].astype(BF16)

    def assemble(rh, ext, inner_at):
        first = lax.broadcasted_iota(jnp.int32, (64, 128), 1) < 64
        verts = (rh[:, VUP : VUP + 384], inner[inner_at, 0], inner[inner_at, 1], rh[:, VDN : VDN + 384])
        above = jnp.where(first, rh[:, CUL : CUL + 128].astype(F32), rh[:, CUR : CUR + 128].astype(F32)).astype(BF16)
        below = jnp.where(first, rh[:, CDL : CDL + 128].astype(F32), rh[:, CDR : CDR + 128].astype(F32)).astype(BF16)
        for s in range(4):
            shift = 128 * (s // 2)
            ext[s, :, 0:384] = verts[s]
            ext[s, :, 384:512] = above if s < 2 else below
            ext[s, :, 512:768] = rh[:, LEFT + shift : LEFT + shift + 256]
            ext[s, :, 768:1024] = rh[:, RIGHT + shift : RIGHT + shift + 256]

    fa[pl.ds(pl.multiple_of(me * 80, 8), 80), :] = ca[me].astype(F32)
    for k in NEAR:
        a_copies[k].wait_recv()
        g = (me + GROUPS - k) % GROUPS
        fa[pl.ds(pl.multiple_of(g * 80, 8), 80), :] = ra[g].astype(F32)
    cell = lax.broadcasted_iota(jnp.int32, (1, 128), 1)
    for b in range(2):
        land = jnp.where((8 * (2 * c + b) + z) * 128 + cell < tally_ref[0], 1.0, 0.0)
        for w in range(W):
            lanes = slice(128 * w, 128 * w + 128)
            h0 = fa[pl.ds(8 * w + b, 16, stride=80), :] + fa[pl.ds(64 + 2 * w + b, 16, stride=80), :]
            parts = [h0 - jnp.sum(h0, axis=0, keepdims=True) * (1.0 / GROUPS)]
            parts += [fa[pl.ds(8 * w + 2 * m + b, 16, stride=80), :] for m in (1, 2, 3)]
            tile = jnp.concatenate(parts, axis=0) * land
            xa[b, :, lanes] = tile.astype(BF16)
    pick(xa, hsa, 0)
    ha_copies = halo(hsa, rha, hs_, hr_)

    fi[pl.ds(pl.multiple_of(me * 64, 8), 64), :] = ci[me].astype(F32)
    for k in NEAR:
        i_copies[k].wait_recv()
        g = (me + GROUPS - k) % GROUPS
        fi[pl.ds(pl.multiple_of(g * 64, 8), 64), :] = ri[g].astype(F32)
    for b in range(2):
        for w in range(W):
            parts = [fi[pl.ds(8 * w + 2 * m + b, 16, stride=64), :] for m in range(4)]
            xi[b, :, 128 * w : 128 * w + 128] = jnp.concatenate(parts, axis=0).astype(BF16)
    pick(xi, hsi, 1)
    hi_copies = halo(hsi, rhi, gs_, gr_)

    for b in range(2):
        for w in range(W):
            turned = xa[b, :, 128 * w : 128 * w + 128].astype(F32).T.astype(BF16)
            at[2 * b, 64 * w : 64 * w + 64, :] = turned[0:64]
            at[2 * b + 1, 64 * w : 64 * w + 64, :] = turned[64:128]
    load_weight.wait()
    for b in range(2):
        @pl.when(4 * (2 * c + b) + z // 2 != me)
        def _(b=b):
            pltpu.make_async_remote_copy(
                src_ref=mask_out.at[0], dst_ref=mask_in.at[b], send_sem=mask_send.at[0], recv_sem=mask_recv.at[b],
                device_id=(t, (me + 1) % GROUPS), device_id_type=MESH,
            ).wait_recv()

    for s in range(4):
        block = s // 2
        region = region_ref[s : s + 1, :]
        row = jnp.zeros((1, 1024), F32)
        for k in ((0, 1, 2, 3, 5), (3, 5, 6, 7, 8), (0, 1, 2, 3, 5), (3, 5, 6, 7, 8))[s]:
            row = jnp.where(region == k, mask_in[block, 0:1, k : k + 1], row)
        weight[s] = weight[s] * row


    def own_taper(s, carry):
        rows = at[s]
        table = selfw_ref[s % 2]
        for n in range(4):
            cov = jnp.dot(rows, xa[s // 2, :, 256 * n : 256 * n + 256], preferred_element_type=F32)
            for h in range(2):
                part = cov[:, 128 * h : 128 * h + 128].reshape(W, 64, 128) * table[None]
                lanes = slice(256 * n + 128 * h, 256 * n + 128 * h + 128)
                tt[s, 0, :, lanes] = part.reshape(512, 128).astype(BF16)
        return carry

    lax.fori_loop(0, 4, own_taper, 0)
    contract = (((1,), (1,)), ((), ()))

    def own_update(s, carry):
        acc[s] = lax.dot_general(tt[s, 0], xi[s // 2], contract, preferred_element_type=F32)
        return carry

    lax.fori_loop(0, 4, own_update, 0)
    for copy in ha_copies:
        copy.wait_recv()
    assemble(rha, exta, 0)

    def halo_taper(s, carry):
        rows = at[s]
        for n in range(4):
            lanes = slice(256 * n, 256 * n + 256)
            cov = jnp.dot(rows, exta[s, :, lanes], preferred_element_type=F32)
            part = cov.reshape(W, 64, 256) * weight[s, :, lanes][None]
            tt[s, 1, :, lanes] = part.reshape(512, 256).astype(BF16)
        return carry

    lax.fori_loop(0, 4, halo_taper, 0)

    for copy in hi_copies:
        copy.wait_recv()
    assemble(rhi, exti, 1)

    def halo_update(s, carry):
        acc[s] = acc[s] + lax.dot_general(tt[s, 1], exti[s], contract, preferred_element_type=F32)
        return carry

    back = {}
    for b in range(2):
        lax.fori_loop(2 * b, 2 * b + 2, halo_update, 0)
        for w in range(W):
            rows = slice(64 * w, 64 * w + 64)
            tile = jnp.concatenate([acc[2 * b, rows, :], acc[2 * b + 1, rows, :]], axis=0).T
            at0 = (8 * b + w) * 64
            rs[at0 : at0 + 64, :] = tile

        def chunk(g, carry, b=b):
            cb[g, b] = rs[pl.ds(512 * b + g, 32, stride=16), :].astype(BF16)
            return carry

        lax.fori_loop(0, GROUPS, chunk, 0)
        for k in NEAR:
            peer = (me + k) % GROUPS
            back[b, k] = pltpu.make_async_remote_copy(
                src_ref=cb.at[peer, b], dst_ref=rb.at[me, b], send_sem=bs_.at[b, k], recv_sem=br_.at[b, k],
                device_id=(t, peer), device_id_type=MESH,
            )
            back[b, k].start()

    for b in range(2):
        fb[pl.ds(pl.multiple_of(me * 64 + 32 * b, 8), 32), :] = cb[me, b].astype(F32)
        for k in NEAR:
            back[b, k].wait_recv()
            g = (me + GROUPS - k) % GROUPS
            fb[pl.ds(pl.multiple_of(g * 64 + 32 * b, 8), 32), :] = rb[g, b].astype(F32)
    for m in range(4):
        for core in range(2):
            for w in range(W):
                pair = [fb[pl.ds(core * 64 + b * 32 + 4 * w + m, 8, stride=128), :] for b in range(2)]
                out_ref[m, 16 * core : 16 * core + 16, 128 * w : 128 * w + 128] = jnp.concatenate(pair, axis=0).astype(BF16)

    for copies in (a_copies, i_copies, back):
        for copy in copies.values():
            copy.wait_send()
    for copy in ha_copies + hi_copies:
        copy.wait_send()
    for q in range(2):
        target, copy = mask_copy(q)

        @pl.when(target != me)
        def _(copy=copy):
            copy.wait_send()


def local(background_draws, scaled_residuals, soil_site_tallies, adjacent_patches, position_kinds):
    select, weights, kinds, self_weights = tables()
    vmem = pl.BlockSpec(memory_space=pltpu.VMEM)
    anywhere = pl.BlockSpec(memory_space=pl.ANY)
    sems = pltpu.SemaphoreType.DMA
    increments = pl.pallas_call(
        kernel,
        out_shape=jax.ShapeDtypeStruct(background_draws.shape, BF16),
        in_specs=[vmem, vmem, pl.BlockSpec(memory_space=pltpu.SMEM), vmem, vmem, vmem, vmem, anywhere],
        out_specs=vmem,
        scratch_shapes=[
            pltpu.VMEM((2, 1024, 1408), BF16),
            pltpu.VMEM((4, 64, 1024), F32),
            pltpu.VMEM((2, 8, 128), F32),
            pltpu.VMEM((2, 8, 128), F32),
            pltpu.VMEM((W, 128, 128), F32),
            pltpu.VMEM((W, 32, 128), F32),
            pltpu.VMEM((W, 128, 128), F32),
            pltpu.VMEM((16, 128), F32),
            pltpu.VMEM((GROUPS, 80, 128), BF16),
            pltpu.VMEM((GROUPS, 64, 128), BF16),
            pltpu.VMEM((GROUPS, 80, 128), BF16),
            pltpu.VMEM((GROUPS, 64, 128), BF16),
            pltpu.VMEM((GROUPS * 80, 128), F32),
            pltpu.VMEM((GROUPS * 64, 128), F32),
            pltpu.VMEM((2, 64, 1024), BF16),
            pltpu.VMEM((2, 64, 1024), BF16),
            pltpu.VMEM((4, 512, 64), BF16),
            pltpu.VMEM((64, 1792), BF16),
            pltpu.VMEM((64, 1792), BF16),
            pltpu.VMEM((64, 2048), BF16),
            pltpu.VMEM((64, 2048), BF16),
            pltpu.VMEM((2, 2, 64, 384), BF16),
            pltpu.VMEM((4, 64, 1024), BF16),
            pltpu.VMEM((4, 64, 1024), BF16),
            pltpu.VMEM((4, 2, 512, 1024), BF16),
            pltpu.VMEM((4, 512, 64), F32),
            pltpu.VMEM((1024, 128), F32),
            pltpu.VMEM((GROUPS, 2, 32, 128), BF16),
            pltpu.VMEM((GROUPS, 2, 32, 128), BF16),
            pltpu.VMEM((GROUPS * 64, 128), F32),
            sems(()), sems((2,)), sems((2,)),
            sems((GROUPS,)), sems((GROUPS,)), sems((GROUPS,)), sems((GROUPS,)),
            sems((8,)), sems((8,)), sems((8,)), sems((8,)),
            sems((2, GROUPS)), sems((2, GROUPS)),
        ],
        compiler_params=pltpu.CompilerParams(
            collective_id=0, has_side_effects=True, vmem_limit_bytes=56 * 2**20
        ),
    )(
        background_draws, scaled_residuals, soil_site_tallies, position_kinds,
        jnp.asarray(kinds), jnp.asarray(self_weights), jnp.asarray(select), jnp.asarray(weights),
    )
    return background_draws + increments.astype(F32)


def solution(mesh):
    in_specs = (
        P("mem", "tile", None),
        P("mem", "tile", None),
        P("tile"),
        P(("tile", "mem"), None),
        P(("tile", "mem"), None),
    )
    out_specs = P("mem", "tile", None)
    return jax.shard_map(local, mesh=mesh, in_specs=in_specs, out_specs=out_specs, check_vma=False)
```

```python
import functools

import jax
import jax.numpy as jnp
import numpy as np
from jax import lax
from jax.experimental import pallas as pl
from jax.experimental.pallas import tpu as pltpu
from jax.sharding import PartitionSpec as P

MESH = pl.DeviceIdType.MESH
F32 = jnp.float32
BF16 = jnp.bfloat16
W = 8
GROUPS = 16
NEAR = [8, 9, 7, 10, 6, 11, 5, 12, 4, 13, 3, 14, 2, 15, 1]


def taper_value(dy, dx):
    dy = np.asarray(dy, np.float32)
    dx = np.asarray(dx, np.float32)
    z = np.sqrt(dx * dx + dy * dy) / np.float32(2)
    near = (((np.float32(-0.25) * z + np.float32(0.5)) * z + np.float32(0.625)) * z - np.float32(5 / 3)) * z * z + 1
    safe = np.maximum(z, np.float32(1))
    far = (
        ((((z / np.float32(12) - np.float32(0.5)) * z + np.float32(0.625)) * z + np.float32(5 / 3)) * z - 5) * z
        + 4
        - np.float32(2) / (3 * safe)
    )
    return np.where(z <= 1, near, np.where(z < 2, far, 0)).astype(np.float32)


def side_slots():
    tiles = [[], [], []]
    for row in range(16):
        for depth in (1, 2, 3):
            tile = 0 if row < 5 else 2 if row > 10 else 1
            if row == 5 and depth == 3:
                tile = 0
            if row == 10 and depth == 3:
                tile = 2
            tiles[tile] += [(row, depth, w) for w in range(W)]
    return tiles


def vert_slots():
    return [(row, col, w) for w in range(W) for row in range(3) for col in range(16)]


def corner_slots():
    return [(a, b, w) for a in (1, 2, 3) for b in (1, 2, 3) if (a, b) != (3, 3) for w in range(W)]


def tables():
    sides, vert, corner = side_slots(), vert_slots(), corner_slots()
    select = np.full((2, 1408), -1, np.int32)

    def put(lane, part, row, col, w):
        block, in_row = divmod(row, 8)
        if part is None or block == part:
            select[block, lane] = w * 128 + in_row * 16 + col

    for lane, (row, col, w) in enumerate(vert):
        put(512 + lane, 0, row, col, w)
        put(1024 + lane, 0, 5 + row, col, w)
        put(512 + lane, 1, 13 + row, col, w)
        put(1024 + lane, 1, 8 + row, col, w)
    for tile in range(3):
        for lane, (row, depth, w) in enumerate(sides[tile]):
            block = row // 8
            at = (tile - block) * 128 + lane
            put(at, block, row, depth - 1, w)
            put(at + 256, block, row, 16 - depth, w)
    for lane, (a, b, w) in enumerate(corner):
        put(896 + lane, 0, a - 1, 16 - b, w)
        put(960 + lane, 0, a - 1, b - 1, w)
        put(896 + lane, 1, 16 - a, 16 - b, w)
        put(960 + lane, 1, 16 - a, b - 1, w)

    weights = np.zeros((4, 64, 1024), np.float32)
    kinds = np.full((4, 1024), 4, np.int32)
    self_weights = np.zeros((2, 64, 128), np.float32)
    cell = np.arange(64)
    for s in range(4):
        block = s // 2
        own_row, own_col = 4 * s + cell // 16, cell % 16
        slots = [None] * 1024
        base = [-3, 8, 5, 16][s]
        for lane, (row, col, w) in enumerate(vert):
            slots[lane] = (base + row, col)
        if s in (0, 3):
            for lane, (a, b, w) in enumerate(corner):
                row = -a if s == 0 else 15 + a
                slots[384 + lane] = (row, -b)
                slots[448 + lane] = (row, 15 + b)
        for k in range(2):
            for lane, (row, depth, w) in enumerate(sides[k + (s >= 2)]):
                slots[512 + 128 * k + lane] = (row, -depth)
                slots[768 + 128 * k + lane] = (row, 15 + depth)
        for lane, slot in enumerate(slots):
            if slot is not None:
                row, col = slot
                weights[s, :, lane] = taper_value(row - own_row, col - own_col) / np.float32(63)
                kinds[s, lane] = 3 * (row // 8 - block + 1) + col // 16 + 1
        if s < 2:
            every = np.arange(128)
            self_weights[s] = taper_value(
                (every // 16)[None] - own_row[:, None], (every % 16)[None] - own_col[:, None]
            ) / np.float32(63)
    return select, weights, kinds, self_weights


UP, DN, TL, TR, CU, CD = 0, 384, 768, 1152, 1536, 1664
VUP, VDN, LEFT, RIGHT, CUL, CUR, CDL, CDR = 0, 384, 768, 1152, 1536, 1664, 1792, 1920


def kernel(
    bg_ref, inn_ref, tally_ref, kinds_ref, region_ref, selfw_ref, select_ref, weight_hbm,
    out_ref,
    sel, weight, mask_out, mask_in, ha, hl, hi, stage, ca, ci, ra, ri, fa, fi, xa, xi, at, hsa, hsi, rha, rhi,
    inner, exta, exti, tt, acc, rs, cb, rb, fb,
    const_sem, mask_send, mask_recv, as_, ar_, is_, ir_, hs_, hr_, gs_, gr_, bs_, br_,
):
    t = lax.axis_index("tile")
    me = lax.axis_index("mem")
    z, c = me // 2, me % 2
    left, right = 2 * ((z + 7) % 8), 2 * ((z + 1) % 8)
    up_tile, down_tile = (t + 15 + c) % 16, (t + c) % 16
    other = 1 - c

    across = (t + 15 + 2 * c) % 16
    barrier = pltpu.get_barrier_semaphore()
    for k in range(1, GROUPS):
        pl.semaphore_signal(barrier, inc=1, device_id=(t, (me + k) % GROUPS), device_id_type=MESH)
    for base in (left, 2 * z, right):
        pl.semaphore_signal(barrier, inc=1, device_id=(across, base + other), device_id_type=MESH)

    load_weight = pltpu.make_async_copy(weight_hbm, weight, const_sem)
    load_weight.start()

    lane8 = lax.broadcasted_iota(jnp.int32, (8, 128), 1)
    for q in range(2):
        held = jnp.where(lane8 == 4, 1.0, 0.0)
        for s in range(9):
            held = jnp.where(kinds_ref[q : q + 1, s : s + 1] == lane8, 1.0, held)
        mask_out[q] = held

    for r in range(4):
        rows = slice(8 * r, 8 * r + 8)
        for w in range(W):
            lanes = slice(128 * w, 128 * w + 128)
            x0, x1, x2, x3 = (bg_ref[m, rows, lanes] for m in range(4))
            s01, d01, s23, d23 = x0 + x1, x0 - x1, x2 + x3, x2 - x3
            h0 = (s01 + s23) * 0.5
            high = h0.astype(BF16).astype(F32)
            base = (r // 2) * 64 + (r % 2) * 8
            ha[w, base : base + 8, :] = high
            ha[w, base + 16 : base + 24, :] = (s01 - s23) * 0.5
            ha[w, base + 32 : base + 40, :] = (d01 + d23) * 0.5
            ha[w, base + 48 : base + 56, :] = (d01 - d23) * 0.5
            hl[w, rows, :] = h0 - high
    def rows_of(source, dest, w):
        return [source[w + n, pl.ds((dest % 2) * 64 + dest // 2, 8, stride=8), :] for n in range(2)]

    def build_a(dest, carry):
        for w in range(0, W, 2):
            ca[dest, 8 * w : 8 * w + 16, :] = jnp.concatenate(rows_of(ha, dest, w), axis=0).astype(BF16)
        for w in range(W):
            stage[2 * w : 2 * w + 2, :] = hl[w, pl.ds((dest % 2) * 16 + dest // 2, 2, stride=8), :]
        ca[dest, 64:80, :] = stage[...].astype(BF16)
        return carry

    lax.fori_loop(0, GROUPS, build_a, 0)

    pl.semaphore_wait(barrier, GROUPS + 2)

    mask_row = me // 4

    def mask_copy(q):
        target = 2 * (2 * (me % 4) + q) + mask_row // 2
        return target, pltpu.make_async_remote_copy(
            src_ref=mask_out.at[q], dst_ref=mask_in.at[mask_row % 2], send_sem=mask_send.at[q],
            recv_sem=mask_recv.at[mask_row % 2], device_id=(t, target), device_id_type=MESH,
        )

    for q in range(2):
        target, copy = mask_copy(q)

        @pl.when(target != me)
        def _(copy=copy):
            copy.start()

        @pl.when(target == me)
        def _(q=q):
            mask_in[mask_row % 2] = mask_out[q]

    def spread(source, landing, send, recv, start=0, size=80):
        copies = {}
        for k in NEAR:
            peer = (me + k) % GROUPS
            copies[k] = pltpu.make_async_remote_copy(
                src_ref=source.at[peer, pl.ds(start, size)], dst_ref=landing.at[me, pl.ds(start, size)],
                send_sem=send.at[k], recv_sem=recv.at[k], device_id=(t, peer), device_id_type=MESH,
            )
            copies[k].start()
        return copies

    a_copies = spread(ca, ra, as_, ar_)
    for w in range(W):
        for m in range(4):
            y = inn_ref[m, :, 128 * w : 128 * w + 128].astype(F32)
            for r in range(4):
                base = (r // 2) * 64 + m * 16 + (r % 2) * 8
                hi[w, base : base + 8, :] = y[8 * r : 8 * r + 8, :]


    def build_i(dest, carry):
        for w in range(0, W, 2):
            ci[dest, 8 * w : 8 * w + 16, :] = jnp.concatenate(rows_of(hi, dest, w), axis=0).astype(BF16)
        return carry

    lax.fori_loop(0, GROUPS, build_i, 0)
    i_copies = spread(ci, ri, is_, ir_, 0, 64)

    for b in range(2):
        wanted = select_ref[b : b + 1, :]

        def one_hot(k, carry, b=b, wanted=wanted):
            entry = lax.broadcasted_iota(jnp.int32, (128, 1408), 0) + 128 * k
            sel[b, pl.ds(pl.multiple_of(128 * k, 128), 128), :] = jnp.where(entry == wanted, 1.0, 0.0).astype(BF16)
            return carry

        lax.fori_loop(0, 8, one_hot, 0)

    def halo(x, hs, rh, send, recv, inner_at):
        copies = []

        def ship(source, landing, width, device, n):
            copy = pltpu.make_async_remote_copy(
                src_ref=hs.at[:, source : source + width], dst_ref=rh.at[:, landing : landing + width],
                send_sem=send.at[n], recv_sem=recv.at[n], device_id=device, device_id_type=MESH,
            )
            copy.start()
            copies.append(copy)

        def pick(b, start, stop):
            return jnp.dot(x[b], sel[b, :, start:stop], preferred_element_type=F32)

        m0, m1 = pick(0, 0, 512), pick(1, 0, 512)
        for k, place in enumerate((TL, TR)):
            at0 = 256 * k
            hs[:, place : place + 128] = m0[:, at0 : at0 + 128].astype(BF16)
            hs[:, place + 128 : place + 256] = (m0[:, at0 + 128 : at0 + 256] + m1[:, at0 : at0 + 128]).astype(BF16)
            hs[:, place + 256 : place + 384] = m1[:, at0 + 128 : at0 + 256].astype(BF16)
        ship(TL, RIGHT, 384, (t, left + c), 3)
        ship(TR, LEFT, 384, (t, right + c), 2)
        m0 = pick(0, 512, 1024).astype(BF16)
        hs[:, UP : UP + 384] = m0[:, 0:384]
        hs[:, CU : CU + 128] = m0[:, 384:512]
        ship(CU, CDL, 128, (up_tile, right + other), 6)
        ship(CU, CDR, 128, (up_tile, left + other), 7)
        ship(UP, VDN, 384, (up_tile, 2 * z + other), 1)
        m1 = pick(1, 512, 1024).astype(BF16)
        hs[:, DN : DN + 384] = m1[:, 0:384]
        hs[:, CD : CD + 128] = m1[:, 384:512]
        ship(CD, CUL, 128, (down_tile, right + other), 4)
        ship(CD, CUR, 128, (down_tile, left + other), 5)
        ship(DN, VUP, 384, (down_tile, 2 * z + other), 0)
        inner[inner_at, 0] = pick(1, 1024, 1408).astype(BF16)
        inner[inner_at, 1] = pick(0, 1024, 1408).astype(BF16)
        return copies

    def sides(rh, ext, inner_at):
        for s in range(4):
            shift = 128 * (s // 2)
            ext[s, :, 512:768] = rh[:, LEFT + shift : LEFT + shift + 256]
            ext[s, :, 768:1024] = rh[:, RIGHT + shift : RIGHT + shift + 256]
        for s in (1, 2):
            ext[s, :, 0:384] = inner[inner_at, s - 1]
            ext[s, :, 384:512] = jnp.zeros((64, 128), BF16)

    def ends(rh, ext):
        first = lax.broadcasted_iota(jnp.int32, (64, 128), 1) < 64
        for s, vert, one, two in ((0, VUP, CUL, CUR), (3, VDN, CDL, CDR)):
            ext[s, :, 0:384] = rh[:, vert : vert + 384]
            corner = jnp.where(first, rh[:, one : one + 128].astype(F32), rh[:, two : two + 128].astype(F32))
            ext[s, :, 384:512] = corner.astype(BF16)

    fa[pl.ds(pl.multiple_of(me * 80, 8), 80), :] = ca[me].astype(F32)
    for k in NEAR:
        a_copies[k].wait_recv()
        g = (me + GROUPS - k) % GROUPS
        fa[pl.ds(pl.multiple_of(g * 80, 8), 80), :] = ra[g].astype(F32)
    cell = lax.broadcasted_iota(jnp.int32, (1, 128), 1)
    for b in range(2):
        land = jnp.where((8 * (2 * c + b) + z) * 128 + cell < tally_ref[0], 1.0, 0.0)
        for w in range(W):
            lanes = slice(128 * w, 128 * w + 128)
            h0 = fa[pl.ds(8 * w + b, 16, stride=80), :] + fa[pl.ds(64 + 2 * w + b, 16, stride=80), :]
            parts = [h0 - jnp.sum(h0, axis=0, keepdims=True) * (1.0 / GROUPS)]
            parts += [fa[pl.ds(8 * w + 2 * m + b, 16, stride=80), :] for m in (1, 2, 3)]
            tile = jnp.concatenate(parts, axis=0) * land
            xa[b, :, lanes] = tile.astype(BF16)
    ha_copies = halo(xa, hsa, rha, hs_, hr_, 0)

    fi[pl.ds(pl.multiple_of(me * 64, 8), 64), :] = ci[me].astype(F32)
    for k in NEAR:
        i_copies[k].wait_recv()
        g = (me + GROUPS - k) % GROUPS
        fi[pl.ds(pl.multiple_of(g * 64, 8), 64), :] = ri[g].astype(F32)
    for b in range(2):
        for w in range(W):
            parts = [fi[pl.ds(8 * w + 2 * m + b, 16, stride=64), :] for m in range(4)]
            xi[b, :, 128 * w : 128 * w + 128] = jnp.concatenate(parts, axis=0).astype(BF16)
    hi_copies = halo(xi, hsi, rhi, gs_, gr_, 1)

    for b in range(2):
        for w in range(W):
            turned = xa[b, :, 128 * w : 128 * w + 128].astype(F32).T.astype(BF16)
            at[2 * b, 64 * w : 64 * w + 64, :] = turned[0:64]
            at[2 * b + 1, 64 * w : 64 * w + 64, :] = turned[64:128]
    load_weight.wait()
    for b in range(2):
        @pl.when(4 * (2 * c + b) + z // 2 != me)
        def _(b=b):
            pltpu.make_async_remote_copy(
                src_ref=mask_out.at[0], dst_ref=mask_in.at[b], send_sem=mask_send.at[0], recv_sem=mask_recv.at[b],
                device_id=(t, (me + 1) % GROUPS), device_id_type=MESH,
            ).wait_recv()

    for s in range(4):
        block = s // 2
        region = region_ref[s : s + 1, :]
        row = jnp.zeros((1, 1024), F32)
        for k in ((0, 1, 2, 3, 5), (3, 5, 6, 7, 8), (0, 1, 2, 3, 5), (3, 5, 6, 7, 8))[s]:
            row = jnp.where(region == k, mask_in[block, 0:1, k : k + 1], row)
        weight[s] = weight[s] * row


    def own_taper(s, carry):
        rows = at[s]
        table = selfw_ref[s % 2]
        for n in range(4):
            cov = jnp.dot(rows, xa[s // 2, :, 256 * n : 256 * n + 256], preferred_element_type=F32)
            for h in range(2):
                part = cov[:, 128 * h : 128 * h + 128].reshape(W, 64, 128) * table[None]
                lanes = slice(256 * n + 128 * h, 256 * n + 128 * h + 128)
                tt[s, 0, :, lanes] = part.reshape(512, 128).astype(BF16)
        return carry

    lax.fori_loop(0, 4, own_taper, 0, unroll=True)
    contract = (((1,), (1,)), ((), ()))

    def own_update(s, carry):
        acc[s] = lax.dot_general(tt[s, 0], xi[s // 2], contract, preferred_element_type=F32)
        return carry

    lax.fori_loop(0, 4, own_update, 0, unroll=True)
    for copy in ha_copies:
        copy.wait_recv()
    sides(rha, exta, 0)
    ends(rha, exta)

    def halo_taper(s, carry):
        rows = at[s]
        for n in range(4):
            lanes = slice(256 * n, 256 * n + 256)
            cov = jnp.dot(rows, exta[s, :, lanes], preferred_element_type=F32)
            part = cov.reshape(W, 64, 256) * weight[s, :, lanes][None]
            tt[s, 1, :, lanes] = part.reshape(512, 256).astype(BF16)
        return carry

    lax.fori_loop(0, 4, halo_taper, 0, unroll=True)

    def halo_update(s, lanes):
        acc[s] = acc[s] + lax.dot_general(tt[s, 1, :, lanes], exti[s, :, lanes], contract, preferred_element_type=F32)

    back = {}

    def give_back(phase, strips):
        for n, s in enumerate(strips):
            for p in range(4):
                at0 = (8 * phase + 4 * n + p) * 64
                rs[at0 : at0 + 64, :] = acc[s, 128 * p : 128 * p + 128, :].T

        def chunk(g, carry):
            cb[g, phase] = rs[pl.ds(512 * phase + g, 32, stride=16), :].astype(BF16)
            return carry

        lax.fori_loop(0, GROUPS, chunk, 0)
        for k in NEAR:
            peer = (me + k) % GROUPS
            back[phase, k] = pltpu.make_async_remote_copy(
                src_ref=cb.at[peer, phase], dst_ref=rb.at[me, phase], send_sem=bs_.at[phase, k],
                recv_sem=br_.at[phase, k], device_id=(t, peer), device_id_type=MESH,
            )
            back[phase, k].start()

    for copy in hi_copies[:2]:
        copy.wait_recv()
    sides(rhi, exti, 1)
    for s in (1, 2):
        halo_update(s, slice(0, 1024))
    give_back(0, (1, 2))
    for s in (0, 3):
        halo_update(s, slice(512, 1024))
    for copy in hi_copies[2:]:
        copy.wait_recv()
    ends(rhi, exti)
    for s in (0, 3):
        halo_update(s, slice(0, 512))
    give_back(1, (0, 3))

    for phase in range(2):
        fb[pl.ds(pl.multiple_of(me * 64 + 32 * phase, 8), 32), :] = cb[me, phase].astype(F32)
        for k in NEAR:
            back[phase, k].wait_recv()
            g = (me + GROUPS - k) % GROUPS
            fb[pl.ds(pl.multiple_of(g * 64 + 32 * phase, 8), 32), :] = rb[g, phase].astype(F32)
    first = lax.broadcasted_iota(jnp.int32, (8, 128), 1) < 64
    place = (32, 0, 16, 48)
    for m in range(4):
        for core in range(2):
            rows = slice(16 * core, 16 * core + 16)
            for p in range(4):
                even, odd = [], []
                for b in range(2):
                    top, low = (
                        fb[pl.ds(core * 64 + place[2 * b + n] + 4 * p + m, 8, stride=128), :] for n in range(2)
                    )
                    even.append(jnp.where(first, top, pltpu.roll(low, 64, 1)))
                    odd.append(jnp.where(first, pltpu.roll(top, 64, 1), low))
                for w, halves in ((2 * p, even), (2 * p + 1, odd)):
                    out_ref[m, rows, 128 * w : 128 * w + 128] = jnp.concatenate(halves, axis=0).astype(BF16)

    for copies in (a_copies, i_copies, back):
        for copy in copies.values():
            copy.wait_send()
    for copy in ha_copies + hi_copies:
        copy.wait_send()
    for q in range(2):
        target, copy = mask_copy(q)

        @pl.when(target != me)
        def _(copy=copy):
            copy.wait_send()


def local(background_draws, scaled_residuals, soil_site_tallies, adjacent_patches, position_kinds):
    select, weights, kinds, self_weights = tables()
    vmem = pl.BlockSpec(memory_space=pltpu.VMEM)
    anywhere = pl.BlockSpec(memory_space=pl.ANY)
    sems = pltpu.SemaphoreType.DMA
    increments = pl.pallas_call(
        kernel,
        out_shape=jax.ShapeDtypeStruct(background_draws.shape, BF16),
        in_specs=[vmem, vmem, pl.BlockSpec(memory_space=pltpu.SMEM), vmem, vmem, vmem, vmem, anywhere],
        out_specs=vmem,
        scratch_shapes=[
            pltpu.VMEM((2, 1024, 1408), BF16),
            pltpu.VMEM((4, 64, 1024), F32),
            pltpu.VMEM((2, 8, 128), F32),
            pltpu.VMEM((2, 8, 128), F32),
            pltpu.VMEM((W, 128, 128), F32),
            pltpu.VMEM((W, 32, 128), F32),
            pltpu.VMEM((W, 128, 128), F32),
            pltpu.VMEM((16, 128), F32),
            pltpu.VMEM((GROUPS, 80, 128), BF16),
            pltpu.VMEM((GROUPS, 64, 128), BF16),
            pltpu.VMEM((GROUPS, 80, 128), BF16),
            pltpu.VMEM((GROUPS, 64, 128), BF16),
            pltpu.VMEM((GROUPS * 80, 128), F32),
            pltpu.VMEM((GROUPS * 64, 128), F32),
            pltpu.VMEM((2, 64, 1024), BF16),
            pltpu.VMEM((2, 64, 1024), BF16),
            pltpu.VMEM((4, 512, 64), BF16),
            pltpu.VMEM((64, 1792), BF16),
            pltpu.VMEM((64, 1792), BF16),
            pltpu.VMEM((64, 2048), BF16),
            pltpu.VMEM((64, 2048), BF16),
            pltpu.VMEM((2, 2, 64, 384), BF16),
            pltpu.VMEM((4, 64, 1024), BF16),
            pltpu.VMEM((4, 64, 1024), BF16),
            pltpu.VMEM((4, 2, 512, 1024), BF16),
            pltpu.VMEM((4, 512, 64), F32),
            pltpu.VMEM((1024, 128), F32),
            pltpu.VMEM((GROUPS, 2, 32, 128), BF16),
            pltpu.VMEM((GROUPS, 2, 32, 128), BF16),
            pltpu.VMEM((GROUPS * 64, 128), F32),
            sems(()), sems((2,)), sems((2,)),
            sems((GROUPS,)), sems((GROUPS,)), sems((GROUPS,)), sems((GROUPS,)),
            sems((8,)), sems((8,)), sems((8,)), sems((8,)),
            sems((2, GROUPS)), sems((2, GROUPS)),
        ],
        compiler_params=pltpu.CompilerParams(
            collective_id=0, has_side_effects=True, vmem_limit_bytes=56 * 2**20
        ),
    )(
        background_draws, scaled_residuals, soil_site_tallies, position_kinds,
        jnp.asarray(kinds), jnp.asarray(self_weights), jnp.asarray(select), jnp.asarray(weights),
    )
    return background_draws + increments.astype(F32)


def solution(mesh):
    in_specs = (
        P("mem", "tile", None),
        P("mem", "tile", None),
        P("tile"),
        P(("tile", "mem"), None),
        P(("tile", "mem"), None),
    )
    out_specs = P("mem", "tile", None)
    return jax.shard_map(local, mesh=mesh, in_specs=in_specs, out_specs=out_specs, check_vma=False)
```

```python
import functools

import jax
import jax.numpy as jnp
import numpy as np
from jax import lax
from jax.experimental import pallas as pl
from jax.experimental.pallas import tpu as pltpu
from jax.sharding import PartitionSpec as P

MESH = pl.DeviceIdType.MESH
F32 = jnp.float32
BF16 = jnp.bfloat16
W = 8
GROUPS = 16
NEAR = [8, 9, 7, 10, 6, 11, 5, 12, 4, 13, 3, 14, 2, 15, 1]


def taper_value(dy, dx):
    dy = np.asarray(dy, np.float32)
    dx = np.asarray(dx, np.float32)
    z = np.sqrt(dx * dx + dy * dy) / np.float32(2)
    near = (((np.float32(-0.25) * z + np.float32(0.5)) * z + np.float32(0.625)) * z - np.float32(5 / 3)) * z * z + 1
    safe = np.maximum(z, np.float32(1))
    far = (
        ((((z / np.float32(12) - np.float32(0.5)) * z + np.float32(0.625)) * z + np.float32(5 / 3)) * z - 5) * z
        + 4
        - np.float32(2) / (3 * safe)
    )
    return np.where(z <= 1, near, np.where(z < 2, far, 0)).astype(np.float32)


def side_places():
    tiles = [[], [], []]
    for row in range(16):
        for depth in (1, 2, 3):
            tile = 0 if row < 5 else 2 if row > 10 else 1
            if row == 5 and depth == 3:
                tile = 0
            if row == 10 and depth == 3:
                tile = 2
            tiles[tile].append((row, depth))
    return tiles


CORNER = [(a, b) for a in (1, 2, 3) for b in (1, 2, 3) if (a, b) != (3, 3)]


def tables():
    sides = side_places()
    select = np.full((2, 768), -1, np.int32)

    def put(block, lane, row, col):
        if row // 8 == block:
            for w in range(4):
                select[block, lane + w] = w * 128 + row % 8 * 16 + col

    for block in range(2):
        for k in range(2):
            for n, (row, depth) in enumerate(sides[k + block]):
                put(block, 64 * k + 4 * n, row, depth - 1)
                put(block, 128 + 64 * k + 4 * n, row, 16 - depth)
        for k in range(3):
            for col in range(16):
                put(block, 256 + 64 * k + 4 * col, 13 * block + k, col)
                put(block, 512 + 64 * k + 4 * col, 5 + 3 * block + k, col)
        for n, (a, b) in enumerate(CORNER):
            row = 16 - a if block else a - 1
            put(block, 448 + 4 * n, row, 16 - b)
            put(block, 480 + 4 * n, row, b - 1)

    weights = np.zeros((4, 64, 1024), np.float32)
    kinds = np.full((4, 1024), 4, np.int32)
    self_weights = np.zeros((2, 64, 128), np.float32)
    cell = np.arange(64)
    for s in range(4):
        block = s // 2
        own_row, own_col = 4 * s + cell // 16, cell % 16

        def place(tile, n, row, col):
            value = taper_value(row - own_row, col - own_col) / np.float32(63)
            for quad in range(2):
                lane = 128 * tile + 64 * quad + 4 * n
                weights[s, :, lane : lane + 4] = value[:, None]
                kinds[s, lane : lane + 4] = 3 * (row // 8 - block + 1) + col // 16 + 1

        for k in range(3):
            for col in range(16):
                place(k, col, (-3, 8, 5, 16)[s] + k, col)
        if s in (0, 3):
            for n, (a, b) in enumerate(CORNER):
                place(3, n, 15 + a if s else -a, -b)
                place(3, 8 + n, 15 + a if s else -a, 15 + b)
        for k in range(2):
            for n, (row, depth) in enumerate(sides[k + block]):
                place(4 + k, n, row, -depth)
                place(6 + k, n, row, 15 + depth)
        if s < 2:
            every = np.arange(128)
            self_weights[s] = taper_value(
                (every // 16)[None] - own_row[:, None], (every % 16)[None] - own_col[:, None]
            ) / np.float32(63)
    return select, weights, kinds, self_weights


UP, DN, TL, TR, CU, CD = 0, 384, 768, 1152, 1536, 1664
VUP, VDN, LEFT, RIGHT, CUL, CUR, CDL, CDR = 0, 384, 768, 1152, 1536, 1664, 1792, 1920


def kernel(
    bg_ref, inn_ref, tally_ref, kinds_ref, region_ref, selfw_ref, select_ref, weight_hbm,
    out_ref,
    sel, weight, mask_out, mask_in, ha, hl, hi, stage, ca, ci, ra, ri, fa, fi, xa, xi, at, hsa, hsi, rha, rhi,
    inner, exta, exti, tt, acc, rs, cb, rb, fb,
    const_sem, mask_send, mask_recv, as_, ar_, is_, ir_, hs_, hr_, gs_, gr_, bs_, br_,
):
    t = lax.axis_index("tile")
    me = lax.axis_index("mem")
    z, c = me // 2, me % 2
    left, right = 2 * ((z + 7) % 8), 2 * ((z + 1) % 8)
    up_tile, down_tile = (t + 15 + c) % 16, (t + c) % 16
    other = 1 - c

    across = (t + 15 + 2 * c) % 16
    barrier = pltpu.get_barrier_semaphore()
    for k in range(1, GROUPS):
        pl.semaphore_signal(barrier, inc=1, device_id=(t, (me + k) % GROUPS), device_id_type=MESH)
    for base in (left, 2 * z, right):
        pl.semaphore_signal(barrier, inc=1, device_id=(across, base + other), device_id_type=MESH)

    load_weight = pltpu.make_async_copy(weight_hbm, weight, const_sem)
    load_weight.start()

    lane8 = lax.broadcasted_iota(jnp.int32, (8, 128), 1)
    for q in range(2):
        held = jnp.where(lane8 == 4, 1.0, 0.0)
        for s in range(9):
            held = jnp.where(kinds_ref[q : q + 1, s : s + 1] == lane8, 1.0, held)
        mask_out[q] = held

    for r in range(4):
        rows = slice(8 * r, 8 * r + 8)
        for w in range(W):
            lanes = slice(128 * w, 128 * w + 128)
            x0, x1, x2, x3 = (bg_ref[m, rows, lanes] for m in range(4))
            s01, d01, s23, d23 = x0 + x1, x0 - x1, x2 + x3, x2 - x3
            h0 = (s01 + s23) * 0.5
            high = h0.astype(BF16).astype(F32)
            base = (r // 2) * 64 + (r % 2) * 8
            ha[w, base : base + 8, :] = high
            ha[w, base + 16 : base + 24, :] = (s01 - s23) * 0.5
            ha[w, base + 32 : base + 40, :] = (d01 + d23) * 0.5
            ha[w, base + 48 : base + 56, :] = (d01 - d23) * 0.5
            hl[w, rows, :] = h0 - high
    def rows_of(source, dest, w):
        return [source[w + n, pl.ds((dest % 2) * 64 + dest // 2, 8, stride=8), :] for n in range(2)]

    def build_a(dest, carry):
        for w in range(0, W, 2):
            ca[dest, 8 * w : 8 * w + 16, :] = jnp.concatenate(rows_of(ha, dest, w), axis=0).astype(BF16)
        for w in range(W):
            stage[2 * w : 2 * w + 2, :] = hl[w, pl.ds((dest % 2) * 16 + dest // 2, 2, stride=8), :]
        ca[dest, 64:80, :] = stage[...].astype(BF16)
        return carry

    lax.fori_loop(0, GROUPS, build_a, 0)

    pl.semaphore_wait(barrier, GROUPS + 2)

    mask_row = me // 4

    def mask_copy(q):
        target = 2 * (2 * (me % 4) + q) + mask_row // 2
        return target, pltpu.make_async_remote_copy(
            src_ref=mask_out.at[q], dst_ref=mask_in.at[mask_row % 2], send_sem=mask_send.at[q],
            recv_sem=mask_recv.at[mask_row % 2], device_id=(t, target), device_id_type=MESH,
        )

    for q in range(2):
        target, copy = mask_copy(q)

        @pl.when(target != me)
        def _(copy=copy):
            copy.start()

        @pl.when(target == me)
        def _(q=q):
            mask_in[mask_row % 2] = mask_out[q]

    def spread(source, landing, send, recv, start=0, size=80):
        copies = {}
        for k in NEAR:
            peer = (me + k) % GROUPS
            copies[k] = pltpu.make_async_remote_copy(
                src_ref=source.at[peer, pl.ds(start, size)], dst_ref=landing.at[me, pl.ds(start, size)],
                send_sem=send.at[k], recv_sem=recv.at[k], device_id=(t, peer), device_id_type=MESH,
            )
            copies[k].start()
        return copies

    a_copies = spread(ca, ra, as_, ar_)
    for w in range(W):
        for m in range(4):
            y = inn_ref[m, :, 128 * w : 128 * w + 128].astype(F32)
            for r in range(4):
                base = (r // 2) * 64 + m * 16 + (r % 2) * 8
                hi[w, base : base + 8, :] = y[8 * r : 8 * r + 8, :]


    def build_i(dest, carry):
        for w in range(0, W, 2):
            ci[dest, 8 * w : 8 * w + 16, :] = jnp.concatenate(rows_of(hi, dest, w), axis=0).astype(BF16)
        return carry

    lax.fori_loop(0, GROUPS, build_i, 0)
    i_copies = spread(ci, ri, is_, ir_, 0, 64)

    for b in range(2):
        wanted = select_ref[b : b + 1, :]

        def one_hot(k, carry, b=b, wanted=wanted):
            entry = lax.broadcasted_iota(jnp.int32, (128, 768), 0) + 128 * k
            sel[b, pl.ds(pl.multiple_of(128 * k, 128), 128), :] = jnp.where(entry == wanted, 1.0, 0.0).astype(BF16)
            return carry

        lax.fori_loop(0, 4, one_hot, 0)

    lower = lane8 < 64

    def halo(x, hs, rh, send, recv, inner_at, start, size):
        rows = slice(start, start + size)
        low = lax.broadcasted_iota(jnp.int32, (size, 128), 1) < 64
        copies = []

        def ship(source, landing, width, device, n):
            copy = pltpu.make_async_remote_copy(
                src_ref=hs.at[rows, source : source + width], dst_ref=rh.at[rows, landing : landing + width],
                send_sem=send.at[n], recv_sem=recv.at[n], device_id=device, device_id_type=MESH,
            )
            copy.start()
            copies.append(copy)

        def pick(b, tiles):
            first, last = 128 * tiles[0], 128 * tiles[-1] + 128
            both = jnp.concatenate([x[b, rows, 0:512], x[b, rows, 512:1024]], axis=0)
            found = jnp.dot(both, sel[b, :, first:last], preferred_element_type=F32)
            out = []
            for n in range(len(tiles)):
                one, two = found[:size, 128 * n : 128 * n + 128], found[size:, 128 * n : 128 * n + 128]
                out.append(jnp.where(low, one, pltpu.roll(two, 64, 1)))
                out.append(jnp.where(low, pltpu.roll(one, 64, 1), two))
            return out

        def put(at0, tile):
            hs[rows, at0 : at0 + 128] = tile.astype(BF16)

        m0, m1 = pick(0, (0, 1)), pick(1, (0, 1))
        for k, place in enumerate((TL, TR)):
            put(place, m0[2 * k])
            put(place + 128, m0[2 * k + 1] + m1[2 * k])
            put(place + 256, m1[2 * k + 1])
        ship(TL, RIGHT, 384, (t, left + c), 3)
        ship(TR, LEFT, 384, (t, right + c), 2)
        for b, vert, corner in ((0, UP, CU), (1, DN, CD)):
            found = pick(b, (2, 3, 4, 5))
            for n in range(3):
                put(vert + 128 * n, found[n])
                inner[inner_at, 1 - b, rows, 128 * n : 128 * n + 128] = found[4 + n].astype(BF16)
            put(corner, found[3])
            tile = down_tile if b else up_tile
            ship(corner, CUL if b else CDL, 128, (tile, right + other), 4 if b else 6)
            ship(corner, CUR if b else CDR, 128, (tile, left + other), 5 if b else 7)
            ship(vert, VUP if b else VDN, 384, (tile, 2 * z + other), 0 if b else 1)
        return copies

    def sides(rh, ext, inner_at):
        for s in range(4):
            shift = 128 * (s // 2)
            ext[s, :, 512:768] = rh[:, LEFT + shift : LEFT + shift + 256]
            ext[s, :, 768:1024] = rh[:, RIGHT + shift : RIGHT + shift + 256]
        for s in (1, 2):
            ext[s, :, 0:384] = inner[inner_at, s - 1]
            ext[s, :, 384:512] = jnp.zeros((64, 128), BF16)

    def ends(rh, ext):
        first = lax.broadcasted_iota(jnp.int32, (64, 128), 1) % 64 < 32
        for s, vert, one, two in ((0, VUP, CUL, CUR), (3, VDN, CDL, CDR)):
            ext[s, :, 0:384] = rh[:, vert : vert + 384]
            corner = jnp.where(first, rh[:, one : one + 128].astype(F32), rh[:, two : two + 128].astype(F32))
            ext[s, :, 384:512] = corner.astype(BF16)

    load_weight.wait()
    for b in range(2):
        @pl.when(4 * (2 * c + b) + z // 2 != me)
        def _(b=b):
            pltpu.make_async_remote_copy(
                src_ref=mask_out.at[0], dst_ref=mask_in.at[b], send_sem=mask_send.at[0], recv_sem=mask_recv.at[b],
                device_id=(t, (me + 1) % GROUPS), device_id_type=MESH,
            ).wait_recv()

    for s in range(4):
        block = s // 2
        region = region_ref[s : s + 1, :]
        row = jnp.zeros((1, 1024), F32)
        for k in ((0, 1, 2, 3, 5), (3, 5, 6, 7, 8), (0, 1, 2, 3, 5), (3, 5, 6, 7, 8))[s]:
            row = jnp.where(region == k, mask_in[block, 0:1, k : k + 1], row)
        weight[s] = weight[s] * row


    fa[pl.ds(pl.multiple_of(me * 80, 8), 80), :] = ca[me].astype(F32)
    for k in NEAR:
        a_copies[k].wait_recv()
        g = (me + GROUPS - k) % GROUPS
        fa[pl.ds(pl.multiple_of(g * 80, 8), 80), :] = ra[g].astype(F32)
    cell = lax.broadcasted_iota(jnp.int32, (1, 128), 1)
    for b in range(2):
        land = jnp.where((8 * (2 * c + b) + z) * 128 + cell < tally_ref[0], 1.0, 0.0)
        for w in range(W):
            lanes = slice(128 * w, 128 * w + 128)
            h0 = fa[pl.ds(8 * w + b, 16, stride=80), :] + fa[pl.ds(64 + 2 * w + b, 16, stride=80), :]
            parts = [h0 - jnp.sum(h0, axis=0, keepdims=True) * (1.0 / GROUPS)]
            parts += [fa[pl.ds(8 * w + 2 * m + b, 16, stride=80), :] for m in (1, 2, 3)]
            tile = jnp.concatenate(parts, axis=0) * land
            xa[b, :, lanes] = tile.astype(BF16)
    ha_copies = halo(xa, hsa, rha, hs_, hr_, 0, 0, 64)

    for b in range(2):
        for w in range(W):
            turned = xa[b, :, 128 * w : 128 * w + 128].astype(F32).T.astype(BF16)
            at[2 * b, 64 * w : 64 * w + 64, :] = turned[0:64]
            at[2 * b + 1, 64 * w : 64 * w + 64, :] = turned[64:128]
    def own_taper(s, carry):
        rows = at[s]
        table = selfw_ref[s % 2]
        for n in range(4):
            cov = jnp.dot(rows, xa[s // 2, :, 256 * n : 256 * n + 256], preferred_element_type=F32)
            for h in range(2):
                part = cov[:, 128 * h : 128 * h + 128].reshape(W, 64, 128) * table[None]
                lanes = slice(256 * n + 128 * h, 256 * n + 128 * h + 128)
                tt[s, 0, :, lanes] = part.reshape(512, 128).astype(BF16)
        return carry

    lax.fori_loop(0, 4, own_taper, 0, unroll=True)
    fi[pl.ds(pl.multiple_of(me * 64, 8), 64), :] = ci[me].astype(F32)
    for k in NEAR:
        i_copies[k].wait_recv()
        g = (me + GROUPS - k) % GROUPS
        fi[pl.ds(pl.multiple_of(g * 64, 8), 64), :] = ri[g].astype(F32)
    for b in range(2):
        for w in range(W):
            parts = [fi[pl.ds(8 * w + 2 * m + b, 16, stride=64), :] for m in range(4)]
            xi[b, :, 128 * w : 128 * w + 128] = jnp.concatenate(parts, axis=0).astype(BF16)
    hi_copies = halo(xi, hsi, rhi, gs_, gr_, 1, 0, 64)

    contract = (((1,), (1,)), ((), ()))

    def own_update(s, carry):
        acc[s] = lax.dot_general(xi[s // 2], tt[s, 0], contract, preferred_element_type=F32)
        return carry

    lax.fori_loop(0, 4, own_update, 0, unroll=True)
    for copy in ha_copies[:2]:
        copy.wait_recv()
    sides(rha, exta, 0)

    def halo_taper(s, carry):
        rows = at[s]
        for n in range(4):
            lanes = slice(256 * n, 256 * n + 256)
            cov = jnp.dot(rows, exta[s, :, lanes], preferred_element_type=F32)
            part = cov.reshape(W, 64, 256) * weight[s, :, lanes][None]
            tt[s, 1, :, lanes] = part.reshape(512, 256).astype(BF16)
        return carry

    for s in (1, 2):
        halo_taper(s, 0)
    for copy in ha_copies[2:]:
        copy.wait_recv()
    ends(rha, exta)
    for s in (0, 3):
        halo_taper(s, 0)

    def halo_update(s, lanes):
        acc[s] = acc[s] + lax.dot_general(exti[s, :, lanes], tt[s, 1, :, lanes], contract, preferred_element_type=F32)

    back = {}

    def give_back(phase, strips):
        for n, s in enumerate(strips):
            for p in range(4):
                at0 = (8 * phase + 4 * n + p) * 64
                rs[at0 : at0 + 64, :] = acc[s, :, 128 * p : 128 * p + 128]

        def chunk(g, carry):
            cb[g, phase] = rs[pl.ds(512 * phase + g, 32, stride=16), :].astype(BF16)
            return carry

        lax.fori_loop(0, GROUPS, chunk, 0, unroll=4)
        for k in NEAR:
            peer = (me + k) % GROUPS
            back[phase, k] = pltpu.make_async_remote_copy(
                src_ref=cb.at[peer, phase], dst_ref=rb.at[me, phase], send_sem=bs_.at[phase, k],
                recv_sem=br_.at[phase, k], device_id=(t, peer), device_id_type=MESH,
            )
            back[phase, k].start()

    for copy in hi_copies[:2]:
        copy.wait_recv()
    sides(rhi, exti, 1)
    for s in (1, 2):
        halo_update(s, slice(0, 1024))
    give_back(0, (1, 2))
    for s in (0, 3):
        halo_update(s, slice(512, 1024))
    for copy in hi_copies[2:]:
        copy.wait_recv()
    ends(rhi, exti)
    for s in (0, 3):
        halo_update(s, slice(0, 512))
    give_back(1, (0, 3))

    for phase in range(2):
        fb[pl.ds(pl.multiple_of(me * 64 + 32 * phase, 8), 32), :] = cb[me, phase].astype(F32)
        for k in NEAR:
            back[phase, k].wait_recv()
            g = (me + GROUPS - k) % GROUPS
            fb[pl.ds(pl.multiple_of(g * 64 + 32 * phase, 8), 32), :] = rb[g, phase].astype(F32)
    first = lax.broadcasted_iota(jnp.int32, (8, 128), 1) < 64
    place = (32, 0, 16, 48)
    for m in range(4):
        for core in range(2):
            rows = slice(16 * core, 16 * core + 16)
            for p in range(4):
                even, odd = [], []
                for b in range(2):
                    top, low = (
                        fb[pl.ds(core * 64 + place[2 * b + n] + 4 * p + m, 8, stride=128), :] for n in range(2)
                    )
                    even.append(jnp.where(first, top, pltpu.roll(low, 64, 1)))
                    odd.append(jnp.where(first, pltpu.roll(top, 64, 1), low))
                for w, halves in ((2 * p, even), (2 * p + 1, odd)):
                    out_ref[m, rows, 128 * w : 128 * w + 128] = jnp.concatenate(halves, axis=0).astype(BF16)

    for copies in (a_copies, i_copies, back):
        for copy in copies.values():
            copy.wait_send()
    for copy in ha_copies + hi_copies:
        copy.wait_send()
    for q in range(2):
        target, copy = mask_copy(q)

        @pl.when(target != me)
        def _(copy=copy):
            copy.wait_send()


def local(background_draws, scaled_residuals, soil_site_tallies, adjacent_patches, position_kinds):
    select, weights, kinds, self_weights = tables()
    vmem = pl.BlockSpec(memory_space=pltpu.VMEM)
    anywhere = pl.BlockSpec(memory_space=pl.ANY)
    sems = pltpu.SemaphoreType.DMA
    increments = pl.pallas_call(
        kernel,
        out_shape=jax.ShapeDtypeStruct(background_draws.shape, BF16),
        in_specs=[vmem, vmem, pl.BlockSpec(memory_space=pltpu.SMEM), vmem, vmem, vmem, vmem, anywhere],
        out_specs=vmem,
        scratch_shapes=[
            pltpu.VMEM((2, 512, 768), BF16),
            pltpu.VMEM((4, 64, 1024), F32),
            pltpu.VMEM((2, 8, 128), F32),
            pltpu.VMEM((2, 8, 128), F32),
            pltpu.VMEM((W, 128, 128), F32),
            pltpu.VMEM((W, 32, 128), F32),
            pltpu.VMEM((W, 128, 128), F32),
            pltpu.VMEM((16, 128), F32),
            pltpu.VMEM((GROUPS, 80, 128), BF16),
            pltpu.VMEM((GROUPS, 64, 128), BF16),
            pltpu.VMEM((GROUPS, 80, 128), BF16),
            pltpu.VMEM((GROUPS, 64, 128), BF16),
            pltpu.VMEM((GROUPS * 80, 128), F32),
            pltpu.VMEM((GROUPS * 64, 128), F32),
            pltpu.VMEM((2, 64, 1024), BF16),
            pltpu.VMEM((2, 64, 1024), BF16),
            pltpu.VMEM((4, 512, 64), BF16),
            pltpu.VMEM((64, 1792), BF16),
            pltpu.VMEM((64, 1792), BF16),
            pltpu.VMEM((64, 2048), BF16),
            pltpu.VMEM((64, 2048), BF16),
            pltpu.VMEM((2, 2, 64, 384), BF16),
            pltpu.VMEM((4, 64, 1024), BF16),
            pltpu.VMEM((4, 64, 1024), BF16),
            pltpu.VMEM((4, 2, 512, 1024), BF16),
            pltpu.VMEM((4, 64, 512), F32),
            pltpu.VMEM((1024, 128), F32),
            pltpu.VMEM((GROUPS, 2, 32, 128), BF16),
            pltpu.VMEM((GROUPS, 2, 32, 128), BF16),
            pltpu.VMEM((GROUPS * 64, 128), F32),
            sems(()), sems((2,)), sems((2,)),
            sems((GROUPS,)), sems((GROUPS,)), sems((GROUPS,)), sems((GROUPS,)),
            sems((8,)), sems((8,)), sems((8,)), sems((8,)),
            sems((2, GROUPS)), sems((2, GROUPS)),
        ],
        compiler_params=pltpu.CompilerParams(
            collective_id=0, has_side_effects=True, vmem_limit_bytes=56 * 2**20
        ),
    )(
        background_draws, scaled_residuals, soil_site_tallies, position_kinds,
        jnp.asarray(kinds), jnp.asarray(self_weights), jnp.asarray(select), jnp.asarray(weights),
    )
    return background_draws + increments.astype(F32)


def solution(mesh):
    in_specs = (
        P("mem", "tile", None),
        P("mem", "tile", None),
        P("tile"),
        P(("tile", "mem"), None),
        P(("tile", "mem"), None),
    )
    out_specs = P("mem", "tile", None)
    return jax.shard_map(local, mesh=mesh, in_specs=in_specs, out_specs=out_specs, check_vma=False)
```

```python
import functools

import jax
import jax.numpy as jnp
import numpy as np
from jax import lax
from jax.experimental import pallas as pl
from jax.experimental.pallas import tpu as pltpu
from jax.sharding import PartitionSpec as P

MESH = pl.DeviceIdType.MESH
F32 = jnp.float32
BF16 = jnp.bfloat16
W = 8
GROUPS = 16
NEAR = [8, 9, 7, 10, 6, 11, 5, 12, 4, 13, 3, 14, 2, 15, 1]


def taper_value(dy, dx):
    dy = np.asarray(dy, np.float32)
    dx = np.asarray(dx, np.float32)
    z = np.sqrt(dx * dx + dy * dy) / np.float32(2)
    near = (((np.float32(-0.25) * z + np.float32(0.5)) * z + np.float32(0.625)) * z - np.float32(5 / 3)) * z * z + 1
    safe = np.maximum(z, np.float32(1))
    far = (
        ((((z / np.float32(12) - np.float32(0.5)) * z + np.float32(0.625)) * z + np.float32(5 / 3)) * z - 5) * z
        + 4
        - np.float32(2) / (3 * safe)
    )
    return np.where(z <= 1, near, np.where(z < 2, far, 0)).astype(np.float32)


def side_places():
    tiles = [[], [], []]
    for row in range(16):
        for depth in (1, 2, 3):
            tile = 0 if row < 5 else 2 if row > 10 else 1
            if row == 5 and depth == 3:
                tile = 0
            if row == 10 and depth == 3:
                tile = 2
            tiles[tile].append((row, depth))
    return tiles


CORNER = [(a, b) for a in (1, 2, 3) for b in (1, 2, 3) if (a, b) != (3, 3)]


def tables():
    sides = side_places()
    select = np.full((2, 768), -1, np.int32)

    def put(block, lane, row, col):
        if row // 8 == block:
            for w in range(4):
                select[block, lane + w] = w * 128 + row % 8 * 16 + col

    for block in range(2):
        for k in range(2):
            for n, (row, depth) in enumerate(sides[k + block]):
                put(block, 64 * k + 4 * n, row, depth - 1)
                put(block, 128 + 64 * k + 4 * n, row, 16 - depth)
        for k in range(3):
            for col in range(16):
                put(block, 256 + 64 * k + 4 * col, 13 * block + k, col)
                put(block, 512 + 64 * k + 4 * col, 5 + 3 * block + k, col)
        for n, (a, b) in enumerate(CORNER):
            row = 16 - a if block else a - 1
            put(block, 448 + 4 * n, row, 16 - b)
            put(block, 480 + 4 * n, row, b - 1)

    weights = np.zeros((4, 64, 1024), np.float32)
    kinds = np.full((4, 1024), 4, np.int32)
    self_weights = np.zeros((2, 64, 128), np.float32)
    cell = np.arange(64)
    for s in range(4):
        block = s // 2
        own_row, own_col = 4 * s + cell // 16, cell % 16

        def place(tile, n, row, col):
            value = taper_value(row - own_row, col - own_col) / np.float32(63)
            for quad in range(2):
                lane = 128 * tile + 64 * quad + 4 * n
                weights[s, :, lane : lane + 4] = value[:, None]
                kinds[s, lane : lane + 4] = 3 * (row // 8 - block + 1) + col // 16 + 1

        for k in range(3):
            for col in range(16):
                place(k, col, (-3, 8, 5, 16)[s] + k, col)
        if s in (0, 3):
            for n, (a, b) in enumerate(CORNER):
                place(3, n, 15 + a if s else -a, -b)
                place(3, 8 + n, 15 + a if s else -a, 15 + b)
        for k in range(2):
            for n, (row, depth) in enumerate(sides[k + block]):
                place(4 + k, n, row, -depth)
                place(6 + k, n, row, 15 + depth)
        if s < 2:
            every = np.arange(128)
            self_weights[s] = taper_value(
                (every // 16)[None] - own_row[:, None], (every % 16)[None] - own_col[:, None]
            ) / np.float32(63)
    return select, weights, kinds, self_weights


UP, DN, TL, TR, CU, CD = 0, 384, 768, 1152, 1536, 1664
VUP, VDN, LEFT, RIGHT, CUL, CUR, CDL, CDR = 0, 384, 768, 1152, 1536, 1664, 1792, 1920


def kernel(
    bg_ref, inn_ref, tally_ref, kinds_ref, region_ref, selfw_ref, select_ref, weight_hbm,
    out_ref,
    sel, weight, mask_out, mask_in, ha, hl, hi, stage, ca, ci, ra, ri, fa, fi, xa, xi, at, hsa, hsi, rha, rhi,
    inner, exta, exti, tt, acc, rs, cb, rb, fb,
    const_sem, mask_send, mask_recv, as_, ar_, is_, ir_, hs_, hr_, gs_, gr_, bs_, br_,
):
    t = lax.axis_index("tile")
    me = lax.axis_index("mem")
    z, c = me // 2, me % 2
    left, right = 2 * ((z + 7) % 8), 2 * ((z + 1) % 8)
    up_tile, down_tile = (t + 15 + c) % 16, (t + c) % 16
    other = 1 - c

    across = (t + 15 + 2 * c) % 16
    barrier = pltpu.get_barrier_semaphore()
    for k in range(1, GROUPS):
        pl.semaphore_signal(barrier, inc=1, device_id=(t, (me + k) % GROUPS), device_id_type=MESH)
    for base in (left, 2 * z, right):
        pl.semaphore_signal(barrier, inc=1, device_id=(across, base + other), device_id_type=MESH)

    load_weight = pltpu.make_async_copy(weight_hbm, weight, const_sem)
    load_weight.start()

    lane8 = lax.broadcasted_iota(jnp.int32, (8, 128), 1)
    for q in range(2):
        held = jnp.where(lane8 == 4, 1.0, 0.0)
        for s in range(9):
            held = jnp.where(kinds_ref[q : q + 1, s : s + 1] == lane8, 1.0, held)
        mask_out[q] = held

    for r in range(4):
        rows = slice(8 * r, 8 * r + 8)
        for w in range(W):
            lanes = slice(128 * w, 128 * w + 128)
            x0, x1, x2, x3 = (bg_ref[m, rows, lanes] for m in range(4))
            s01, d01, s23, d23 = x0 + x1, x0 - x1, x2 + x3, x2 - x3
            h0 = (s01 + s23) * 0.5
            high = h0.astype(BF16).astype(F32)
            base = (r // 2) * 64 + (r % 2) * 8
            ha[w, base : base + 8, :] = high
            ha[w, base + 16 : base + 24, :] = (s01 - s23) * 0.5
            ha[w, base + 32 : base + 40, :] = (d01 + d23) * 0.5
            ha[w, base + 48 : base + 56, :] = (d01 - d23) * 0.5
            hl[w, rows, :] = h0 - high
    def rows_of(source, dest, w):
        return [source[w + n, pl.ds((dest % 2) * 64 + dest // 2, 8, stride=8), :] for n in range(2)]

    def build_a(dest, carry):
        for w in range(0, W, 2):
            ca[dest, 8 * w : 8 * w + 16, :] = jnp.concatenate(rows_of(ha, dest, w), axis=0).astype(BF16)
        for w in range(W):
            stage[2 * w : 2 * w + 2, :] = hl[w, pl.ds((dest % 2) * 16 + dest // 2, 2, stride=8), :]
        ca[dest, 64:80, :] = stage[...].astype(BF16)
        return carry

    lax.fori_loop(0, GROUPS, build_a, 0)

    pl.semaphore_wait(barrier, GROUPS + 2)

    mask_row = me // 4

    def mask_copy(q):
        target = 2 * (2 * (me % 4) + q) + mask_row // 2
        return target, pltpu.make_async_remote_copy(
            src_ref=mask_out.at[q], dst_ref=mask_in.at[mask_row % 2], send_sem=mask_send.at[q],
            recv_sem=mask_recv.at[mask_row % 2], device_id=(t, target), device_id_type=MESH,
        )

    for q in range(2):
        target, copy = mask_copy(q)

        @pl.when(target != me)
        def _(copy=copy):
            copy.start()

        @pl.when(target == me)
        def _(q=q):
            mask_in[mask_row % 2] = mask_out[q]

    def spread(source, landing, send, recv, start=0, size=80):
        copies = {}
        for k in NEAR:
            peer = (me + k) % GROUPS
            copies[k] = pltpu.make_async_remote_copy(
                src_ref=source.at[peer, pl.ds(start, size)], dst_ref=landing.at[me, pl.ds(start, size)],
                send_sem=send.at[k], recv_sem=recv.at[k], device_id=(t, peer), device_id_type=MESH,
            )
            copies[k].start()
        return copies

    a_copies = spread(ca, ra, as_, ar_)
    for w in range(W):
        for m in range(4):
            y = inn_ref[m, :, 128 * w : 128 * w + 128].astype(F32)
            for r in range(4):
                base = (r // 2) * 64 + m * 16 + (r % 2) * 8
                hi[w, base : base + 8, :] = y[8 * r : 8 * r + 8, :]


    def build_i(dest, carry):
        for w in range(0, W, 2):
            ci[dest, 8 * w : 8 * w + 16, :] = jnp.concatenate(rows_of(hi, dest, w), axis=0).astype(BF16)
        return carry

    lax.fori_loop(0, GROUPS, build_i, 0)
    i_copies = spread(ci, ri, is_, ir_, 0, 64)

    for b in range(2):
        wanted = select_ref[b : b + 1, :]

        def one_hot(k, carry, b=b, wanted=wanted):
            entry = lax.broadcasted_iota(jnp.int32, (128, 768), 0) + 128 * k
            sel[b, pl.ds(pl.multiple_of(128 * k, 128), 128), :] = jnp.where(entry == wanted, 1.0, 0.0).astype(BF16)
            return carry

        lax.fori_loop(0, 4, one_hot, 0)

    lower = lane8 < 64

    def halo(x, hs, rh, send, recv, inner_at, start, size):
        rows = slice(start, start + size)
        low = lax.broadcasted_iota(jnp.int32, (size, 128), 1) < 64
        copies = []

        def ship(source, landing, width, device, n):
            copy = pltpu.make_async_remote_copy(
                src_ref=hs.at[rows, source : source + width], dst_ref=rh.at[rows, landing : landing + width],
                send_sem=send.at[n], recv_sem=recv.at[n], device_id=device, device_id_type=MESH,
            )
            copy.start()
            copies.append(copy)

        def pick(b, tiles):
            first, last = 128 * tiles[0], 128 * tiles[-1] + 128
            both = jnp.concatenate([x[b, rows, 0:512], x[b, rows, 512:1024]], axis=0)
            found = jnp.dot(both, sel[b, :, first:last], preferred_element_type=F32)
            out = []
            for n in range(len(tiles)):
                one, two = found[:size, 128 * n : 128 * n + 128], found[size:, 128 * n : 128 * n + 128]
                out.append(jnp.where(low, one, pltpu.roll(two, 64, 1)))
                out.append(jnp.where(low, pltpu.roll(one, 64, 1), two))
            return out

        def put(at0, tile):
            hs[rows, at0 : at0 + 128] = tile.astype(BF16)

        for b, vert, corner in ((0, UP, CU), (1, DN, CD)):
            found = pick(b, (2, 3, 4, 5))
            for n in range(3):
                put(vert + 128 * n, found[n])
                inner[inner_at, 1 - b, rows, 128 * n : 128 * n + 128] = found[4 + n].astype(BF16)
            put(corner, found[3])
            tile = down_tile if b else up_tile
            ship(corner, CUL if b else CDL, 128, (tile, right + other), 4 if b else 6)
            ship(corner, CUR if b else CDR, 128, (tile, left + other), 5 if b else 7)
            ship(vert, VUP if b else VDN, 384, (tile, 2 * z + other), 0 if b else 1)
        m0, m1 = pick(0, (0, 1)), pick(1, (0, 1))
        for k, place in enumerate((TL, TR)):
            put(place, m0[2 * k])
            put(place + 128, m0[2 * k + 1] + m1[2 * k])
            put(place + 256, m1[2 * k + 1])
        ship(TL, RIGHT, 384, (t, left + c), 3)
        ship(TR, LEFT, 384, (t, right + c), 2)
        return copies

    def sides(rh, ext, inner_at):
        for s in range(4):
            shift = 128 * (s // 2)
            ext[s, :, 512:768] = rh[:, LEFT + shift : LEFT + shift + 256]
            ext[s, :, 768:1024] = rh[:, RIGHT + shift : RIGHT + shift + 256]
        for s in (1, 2):
            ext[s, :, 0:384] = inner[inner_at, s - 1]
            ext[s, :, 384:512] = jnp.zeros((64, 128), BF16)

    def ends(rh, ext):
        first = lax.broadcasted_iota(jnp.int32, (64, 128), 1) % 64 < 32
        for s, vert, one, two in ((0, VUP, CUL, CUR), (3, VDN, CDL, CDR)):
            ext[s, :, 0:384] = rh[:, vert : vert + 384]
            corner = jnp.where(first, rh[:, one : one + 128].astype(F32), rh[:, two : two + 128].astype(F32))
            ext[s, :, 384:512] = corner.astype(BF16)

    load_weight.wait()
    for b in range(2):
        @pl.when(4 * (2 * c + b) + z // 2 != me)
        def _(b=b):
            pltpu.make_async_remote_copy(
                src_ref=mask_out.at[0], dst_ref=mask_in.at[b], send_sem=mask_send.at[0], recv_sem=mask_recv.at[b],
                device_id=(t, (me + 1) % GROUPS), device_id_type=MESH,
            ).wait_recv()

    for s in range(4):
        block = s // 2
        region = region_ref[s : s + 1, :]
        row = jnp.zeros((1, 1024), F32)
        for k in ((0, 1, 2, 3, 5), (3, 5, 6, 7, 8), (0, 1, 2, 3, 5), (3, 5, 6, 7, 8))[s]:
            row = jnp.where(region == k, mask_in[block, 0:1, k : k + 1], row)
        weight[s] = weight[s] * row


    fa[pl.ds(pl.multiple_of(me * 80, 8), 80), :] = ca[me].astype(F32)
    for k in NEAR:
        a_copies[k].wait_recv()
        g = (me + GROUPS - k) % GROUPS
        fa[pl.ds(pl.multiple_of(g * 80, 8), 80), :] = ra[g].astype(F32)
    cell = lax.broadcasted_iota(jnp.int32, (1, 128), 1)
    for b in range(2):
        land = jnp.where((8 * (2 * c + b) + z) * 128 + cell < tally_ref[0], 1.0, 0.0)
        for w in range(W):
            lanes = slice(128 * w, 128 * w + 128)
            h0 = fa[pl.ds(8 * w + b, 16, stride=80), :] + fa[pl.ds(64 + 2 * w + b, 16, stride=80), :]
            parts = [h0 - jnp.sum(h0, axis=0, keepdims=True) * (1.0 / GROUPS)]
            parts += [fa[pl.ds(8 * w + 2 * m + b, 16, stride=80), :] for m in (1, 2, 3)]
            tile = jnp.concatenate(parts, axis=0) * land
            xa[b, :, lanes] = tile.astype(BF16)
    ha_copies = halo(xa, hsa, rha, hs_, hr_, 0, 0, 64)

    for b in range(2):
        for w in range(W):
            turned = xa[b, :, 128 * w : 128 * w + 128].astype(F32).T.astype(BF16)
            at[2 * b, 64 * w : 64 * w + 64, :] = turned[0:64]
            at[2 * b + 1, 64 * w : 64 * w + 64, :] = turned[64:128]
    def own_taper(s, carry):
        rows = at[s]
        table = selfw_ref[s % 2]
        for n in range(4):
            cov = jnp.dot(rows, xa[s // 2, :, 256 * n : 256 * n + 256], preferred_element_type=F32)
            for h in range(2):
                part = cov[:, 128 * h : 128 * h + 128].reshape(W, 64, 128) * table[None]
                lanes = slice(256 * n + 128 * h, 256 * n + 128 * h + 128)
                tt[s, 0, :, lanes] = part.reshape(512, 128).astype(BF16)
        return carry

    lax.fori_loop(0, 4, own_taper, 0, unroll=True)
    fi[pl.ds(pl.multiple_of(me * 64, 8), 64), :] = ci[me].astype(F32)
    for k in NEAR:
        i_copies[k].wait_recv()
        g = (me + GROUPS - k) % GROUPS
        fi[pl.ds(pl.multiple_of(g * 64, 8), 64), :] = ri[g].astype(F32)
    for b in range(2):
        for w in range(W):
            parts = [fi[pl.ds(8 * w + 2 * m + b, 16, stride=64), :] for m in range(4)]
            xi[b, :, 128 * w : 128 * w + 128] = jnp.concatenate(parts, axis=0).astype(BF16)
    hi_copies = halo(xi, hsi, rhi, gs_, gr_, 1, 0, 64)

    contract = (((1,), (1,)), ((), ()))

    def own_update(s, carry):
        acc[s] = lax.dot_general(xi[s // 2], tt[s, 0], contract, preferred_element_type=F32)
        return carry

    lax.fori_loop(0, 4, own_update, 0, unroll=True)
    for copy in ha_copies[6:]:
        copy.wait_recv()
    sides(rha, exta, 0)

    def halo_taper(s, carry):
        rows = at[s]
        for n in range(4):
            lanes = slice(256 * n, 256 * n + 256)
            cov = jnp.dot(rows, exta[s, :, lanes], preferred_element_type=F32)
            part = cov.reshape(W, 64, 256) * weight[s, :, lanes][None]
            tt[s, 1, :, lanes] = part.reshape(512, 256).astype(BF16)
        return carry

    for s in (1, 2):
        halo_taper(s, 0)
    for copy in ha_copies[:6]:
        copy.wait_recv()
    ends(rha, exta)
    for s in (0, 3):
        halo_taper(s, 0)

    def halo_update(s, lanes):
        acc[s] = acc[s] + lax.dot_general(exti[s, :, lanes], tt[s, 1, :, lanes], contract, preferred_element_type=F32)

    back = {}

    def give_back(phase, strips):
        for n, s in enumerate(strips):
            for p in range(4):
                at0 = (8 * phase + 4 * n + p) * 64
                rs[at0 : at0 + 64, :] = acc[s, :, 128 * p : 128 * p + 128]

        def chunk(g, carry):
            cb[g, phase] = rs[pl.ds(512 * phase + g, 32, stride=16), :].astype(BF16)
            return carry

        lax.fori_loop(0, GROUPS, chunk, 0, unroll=4)
        for k in NEAR:
            peer = (me + k) % GROUPS
            back[phase, k] = pltpu.make_async_remote_copy(
                src_ref=cb.at[peer, phase], dst_ref=rb.at[me, phase], send_sem=bs_.at[phase, k],
                recv_sem=br_.at[phase, k], device_id=(t, peer), device_id_type=MESH,
            )
            back[phase, k].start()

    for copy in hi_copies[6:]:
        copy.wait_recv()
    sides(rhi, exti, 1)
    for s in (1, 2):
        halo_update(s, slice(0, 1024))
    give_back(0, (1, 2))
    for s in (0, 3):
        halo_update(s, slice(512, 1024))
    for copy in hi_copies[:6]:
        copy.wait_recv()
    ends(rhi, exti)
    for s in (0, 3):
        halo_update(s, slice(0, 512))
    give_back(1, (0, 3))

    for phase in range(2):
        fb[pl.ds(pl.multiple_of(me * 64 + 32 * phase, 8), 32), :] = cb[me, phase].astype(F32)
        for k in NEAR:
            back[phase, k].wait_recv()
            g = (me + GROUPS - k) % GROUPS
            fb[pl.ds(pl.multiple_of(g * 64 + 32 * phase, 8), 32), :] = rb[g, phase].astype(F32)
    first = lax.broadcasted_iota(jnp.int32, (8, 128), 1) < 64
    place = (32, 0, 16, 48)
    for m in range(4):
        for core in range(2):
            rows = slice(16 * core, 16 * core + 16)
            for p in range(4):
                even, odd = [], []
                for b in range(2):
                    top, low = (
                        fb[pl.ds(core * 64 + place[2 * b + n] + 4 * p + m, 8, stride=128), :] for n in range(2)
                    )
                    even.append(jnp.where(first, top, pltpu.roll(low, 64, 1)))
                    odd.append(jnp.where(first, pltpu.roll(top, 64, 1), low))
                for w, halves in ((2 * p, even), (2 * p + 1, odd)):
                    out_ref[m, rows, 128 * w : 128 * w + 128] = jnp.concatenate(halves, axis=0).astype(BF16)

    for copies in (a_copies, i_copies, back):
        for copy in copies.values():
            copy.wait_send()
    for copy in ha_copies + hi_copies:
        copy.wait_send()
    for q in range(2):
        target, copy = mask_copy(q)

        @pl.when(target != me)
        def _(copy=copy):
            copy.wait_send()


def local(background_draws, scaled_residuals, soil_site_tallies, adjacent_patches, position_kinds):
    select, weights, kinds, self_weights = tables()
    vmem = pl.BlockSpec(memory_space=pltpu.VMEM)
    anywhere = pl.BlockSpec(memory_space=pl.ANY)
    sems = pltpu.SemaphoreType.DMA
    increments = pl.pallas_call(
        kernel,
        out_shape=jax.ShapeDtypeStruct(background_draws.shape, BF16),
        in_specs=[vmem, vmem, pl.BlockSpec(memory_space=pltpu.SMEM), vmem, vmem, vmem, vmem, anywhere],
        out_specs=vmem,
        scratch_shapes=[
            pltpu.VMEM((2, 512, 768), BF16),
            pltpu.VMEM((4, 64, 1024), F32),
            pltpu.VMEM((2, 8, 128), F32),
            pltpu.VMEM((2, 8, 128), F32),
            pltpu.VMEM((W, 128, 128), F32),
            pltpu.VMEM((W, 32, 128), F32),
            pltpu.VMEM((W, 128, 128), F32),
            pltpu.VMEM((16, 128), F32),
            pltpu.VMEM((GROUPS, 80, 128), BF16),
            pltpu.VMEM((GROUPS, 64, 128), BF16),
            pltpu.VMEM((GROUPS, 80, 128), BF16),
            pltpu.VMEM((GROUPS, 64, 128), BF16),
            pltpu.VMEM((GROUPS * 80, 128), F32),
            pltpu.VMEM((GROUPS * 64, 128), F32),
            pltpu.VMEM((2, 64, 1024), BF16),
            pltpu.VMEM((2, 64, 1024), BF16),
            pltpu.VMEM((4, 512, 64), BF16),
            pltpu.VMEM((64, 1792), BF16),
            pltpu.VMEM((64, 1792), BF16),
            pltpu.VMEM((64, 2048), BF16),
            pltpu.VMEM((64, 2048), BF16),
            pltpu.VMEM((2, 2, 64, 384), BF16),
            pltpu.VMEM((4, 64, 1024), BF16),
            pltpu.VMEM((4, 64, 1024), BF16),
            pltpu.VMEM((4, 2, 512, 1024), BF16),
            pltpu.VMEM((4, 64, 512), F32),
            pltpu.VMEM((1024, 128), F32),
            pltpu.VMEM((GROUPS, 2, 32, 128), BF16),
            pltpu.VMEM((GROUPS, 2, 32, 128), BF16),
            pltpu.VMEM((GROUPS * 64, 128), F32),
            sems(()), sems((2,)), sems((2,)),
            sems((GROUPS,)), sems((GROUPS,)), sems((GROUPS,)), sems((GROUPS,)),
            sems((8,)), sems((8,)), sems((8,)), sems((8,)),
            sems((2, GROUPS)), sems((2, GROUPS)),
        ],
        compiler_params=pltpu.CompilerParams(
            collective_id=0, has_side_effects=True, vmem_limit_bytes=56 * 2**20
        ),
    )(
        background_draws, scaled_residuals, soil_site_tallies, position_kinds,
        jnp.asarray(kinds), jnp.asarray(self_weights), jnp.asarray(select), jnp.asarray(weights),
    )
    return background_draws + increments.astype(F32)


def solution(mesh):
    in_specs = (
        P("mem", "tile", None),
        P("mem", "tile", None),
        P("tile"),
        P(("tile", "mem"), None),
        P(("tile", "mem"), None),
    )
    out_specs = P("mem", "tile", None)
    return jax.shard_map(local, mesh=mesh, in_specs=in_specs, out_specs=out_specs, check_vma=False)
```
